512 devices in a mesh: lat: 32 (over x_hi, y, core), lon: 16 (over z, x_lo).
Axes of the slice: x: 4 (x_hi: 2, x_lo: 2; x = x_hi * 2 + x_lo), y: 8, z: 8, core: 2. Of those that a mesh axis runs over, the one named last changes fastest.
Arguments:
- flow_state: float32 [5, 9, 4, 512, 2048], P(None, None, None, 'lat', 'lon'), may hold values from -8 to 8
- jacobian_lat: float32 [5, 5], replicated, may hold values from -2.5 to 2.5
- jacobian_lon: float32 [5, 5], replicated, may hold values from -2.5 to 2.5
- jacobian_rad: float32 [5, 5], replicated, may hold values from -2.5 to 2.5
- ratio_real: float32 [256, 5], replicated, may hold values from -1.5 to -0.3
- ratio_imag: float32 [256, 4], replicated, may hold values from -1 to 1
- degree_cut: int32 [5], replicated, may hold values from 128 to 255, as said below
Outputs:
- residual: float32 [5, 9, 4, 512, 2048], P(None, None, None, 'lat', 'lon')
- normal_derivative: float32 [5, 9, 512, 2048], P(None, None, 'lat', 'lon')
The draws below stay inside these ranges and needn't reach their ends.
Inputs may be any that keep to these rules, and one draw needn't show every extreme that they name: degree_cut[n] is the highest degree kept at time frequency n.
All inputs are finite; a program needn't handle non-finite values.
Results may differ from the reference program's by a relative error of at most 0.001.
Values sent between devices are 32-bit elements; how exact they have to be, the bound alone decides.
A program may use at most 128 MiB of HBM per device.

```python
import math
import jax
import jax.numpy as jnp
from jax import lax

VARS = 5
INST = 9
RAD = 4
NLAT = 512
NLON = 2048
MODES = 256
FIELDS = 45
NFREQ = 5
NPAIR = 4


def draw_flow_state(key, part):
    key = jax.random.fold_in(key, 11)
    keys = jax.random.split(key, 3)
    shape = (VARS, INST, RAD, NLAT, NLON)
    lat_scale = jnp.exp(jax.random.uniform(keys[1], (NLAT,), jnp.float32, -0.57, 0.57))
    lon_scale = jnp.exp(jax.random.uniform(keys[2], (NLON,), jnp.float32, -0.57, 0.57))
    scale = lat_scale[:, None] * lon_scale[None, :]
    noise = jnp.clip(jax.random.normal(keys[0], shape, jnp.float32), -2.5, 2.5)
    return noise * scale


def draw_degree_cut(key, part):
    key = jax.random.fold_in(key, 23)
    keys = jax.random.split(key, 2)
    cuts = jax.random.randint(keys[0], (NFREQ,), MODES // 2, MODES, jnp.int32)
    cuts = cuts.at[0].set(MODES - 1).at[1].set(MODES // 2)
    return cuts[jax.random.permutation(keys[1], NFREQ)]


def centred(own_key, extent, scale, bound, kind=jnp.bfloat16):
    array = scale * jax.random.normal(own_key, extent, jnp.float32)
    return jnp.clip(array, min=-bound, max=bound).astype(kind)


def setup_inputs(seed: int = 0) -> dict:
    splits = jax.random.split(jax.random.key(seed), 8)
    return {
        "flow_state": draw_flow_state(jax.random.fold_in(splits[7], 71), 0),
        "jacobian_lat": centred(splits[1], (VARS, VARS), VARS ** -0.5, 2.5, jnp.float32),
        "jacobian_lon": centred(splits[2], (VARS, VARS), VARS ** -0.5, 2.5, jnp.float32),
        "jacobian_rad": centred(splits[3], (VARS, VARS), VARS ** -0.5, 2.5, jnp.float32),
        "ratio_real": jnp.clip(jax.random.uniform(splits[4], (MODES, NFREQ), jnp.float32, -1.5, -0.3), -1.5, -0.3),
        "ratio_imag": jnp.clip(jax.random.uniform(splits[5], (MODES, NPAIR), jnp.float32, -1.0, 1.0), -1.0, 1.0),
        "degree_cut": draw_degree_cut(jax.random.fold_in(splits[7], 71), 0),
    }


damping = 0.5
highest = lax.Precision.HIGHEST
start_floor = -36.0

def fejer_weights(lat_index, total_rows):
    series_terms = jnp.arange(1, total_rows // 2 + 1, dtype=jnp.int32)
    phase_index = series_terms[None, :] * (2 * lat_index[:, None] + 1) % (2 * total_rows)
    angles = phase_index.astype(jnp.float32) * (math.pi / total_rows)
    divisor = (4 * series_terms * series_terms - 1).astype(jnp.float32)
    series = lax.optimization_barrier(jnp.sum(jnp.cos(angles) / divisor[None, :], axis=1))
    return 2.0 / total_rows * (1.0 - 2.0 * series)

def legendre_matrix(orders, colatitude, harmonic_degree_total):
    cosine = jnp.cos(colatitude)[None, :]
    order_f = orders.astype(jnp.float32)[:, None]
    log_start = 0.5 * (jnp.log((2.0 * order_f + 1.0) / (4.0 * math.pi)) + lax.lgamma(order_f + 0.5) - lax.lgamma(order_f + 1.0) - 0.5 * math.log(math.pi))
    log_diagonal = log_start + order_f * jnp.log(jnp.sin(colatitude))[None, :]
    diagonal = jnp.where(log_diagonal >= start_floor, jnp.exp(jnp.maximum(log_diagonal, start_floor)), 0.0)

    def advance(state_pair, degree):
        latest, before = state_pair
        degree_f = degree.astype(jnp.float32)
        factor = jnp.sqrt(jnp.maximum(4.0 * degree_f * degree_f - 1.0, 1.0) / jnp.maximum(degree_f * degree_f - order_f * order_f, 1.0))
        degree_prev = degree_f - 1.0
        factor_prev = jnp.sqrt(jnp.maximum(4.0 * degree_prev * degree_prev - 1.0, 1.0) / jnp.maximum(degree_prev * degree_prev - order_f * order_f, 1.0))
        quotient = jnp.where(degree_prev > order_f, factor / factor_prev, 0.0)
        grown = factor * cosine * latest - quotient * before
        fresh_row = jnp.where(degree_f == order_f, diagonal, jnp.where(degree_f > order_f, grown, 0.0))
        return ((fresh_row, latest), fresh_row)
    zero_rows = jnp.zeros_like(diagonal)
    _, legendre = lax.scan(advance, (zero_rows, zero_rows), jnp.arange(harmonic_degree_total, dtype=jnp.int32), unroll=16)
    return legendre

def instance_kernel(ratio_real, ratio_imag, degree_cut, first_degree, amount):
    sample_moment_number = 2 * ratio_imag.shape[1] + 1
    degree = first_degree + jnp.arange(amount, dtype=jnp.int32)
    keep = (degree[:, None] <= degree_cut[None, :]).astype(jnp.float32)
    real_part = lax.dynamic_slice_in_dim(ratio_real, first_degree, amount, 0) * keep
    imag_part = lax.dynamic_slice_in_dim(ratio_imag, first_degree, amount, 0) * keep[:, 1:]
    period_sample_points = jnp.arange(sample_moment_number, dtype=jnp.int32)
    moment_shift_lag = period_sample_points[:, None] - period_sample_points[None, :]
    harmonic = jnp.arange(1, ratio_real.shape[1], dtype=jnp.int32)
    phase_index = harmonic[:, None, None] * moment_shift_lag[None] % sample_moment_number
    angles = phase_index.astype(jnp.float32) * (2.0 * math.pi / sample_moment_number)
    kernel = real_part[:, :1, None] + 2.0 * jnp.einsum('ln,nts->lts', real_part[:, 1:], jnp.cos(angles), precision=highest) - 2.0 * jnp.einsum('ln,nts->lts', imag_part, jnp.sin(angles), precision=highest)
    return kernel / sample_moment_number

def spectral_matrix(sample_moment_number):
    period_sample_points = jnp.arange(sample_moment_number, dtype=jnp.int32)
    moment_shift_lag = period_sample_points[:, None] - period_sample_points[None, :]
    parity = jnp.where(moment_shift_lag % 2 == 0, 1.0, -1.0).astype(jnp.float32)
    safe_lag = jnp.where(moment_shift_lag == 0, 1, moment_shift_lag).astype(jnp.float32)
    return jnp.where(moment_shift_lag == 0, 0.0, 0.5 * parity / jnp.sin(math.pi * safe_lag / sample_moment_number)).astype(jnp.float32)

def mix_vars(matrix, difference):
    return jnp.einsum('vw,w...->v...', matrix, difference, precision=highest)

def layer_residual(centre, inner_layer, outer_layer, north_row, south_row, west_col, east_col, sine_lat, jacobian_lat, jacobian_lon, jacobian_rad):
    flux_sum = sine_lat * (mix_vars(jacobian_lat, 0.5 * (south_row - north_row)) + mix_vars(jacobian_rad, 0.5 * (outer_layer - inner_layer))) + mix_vars(jacobian_lon, 0.5 * (east_col - west_col))
    spread = sine_lat * (south_row + north_row + outer_layer + inner_layer - 4.0 * centre) + (east_col + west_col - 2.0 * centre)
    timing = jnp.einsum('ts,vs...->vt...', spectral_matrix(centre.shape[1]), centre, precision=highest)
    return timing + flux_sum - damping * spread

def reference(flow_state, jacobian_lat, jacobian_lon, jacobian_rad, ratio_real, ratio_imag, degree_cut):
    lat_index = jnp.arange(NLAT, dtype=jnp.int32)
    colatitude = (lat_index.astype(jnp.float32) + 0.5) * (math.pi / NLAT)
    weights = fejer_weights(lat_index, NLAT)
    legendre = legendre_matrix(jnp.arange(MODES, dtype=jnp.int32), colatitude, MODES)
    farfield_shell = flow_state[:, :, RAD - 1].reshape(FIELDS, NLAT, NLON)
    spectrum = jnp.fft.rfft(farfield_shell, axis=-1)[..., :MODES]
    fourier = jnp.stack([jnp.real(spectrum), jnp.imag(spectrum)], axis=1) * (2.0 * math.pi / NLON)
    fourier = fourier * weights[None, None, :, None]
    coefficients = jnp.einsum('lmj,fcjm->lmfc', legendre, fourier, precision=highest)
    kernel = instance_kernel(ratio_real, ratio_imag, degree_cut, 0, MODES)
    shaped = coefficients.reshape(MODES, MODES, VARS, INST, 2)
    bent_coef = jnp.einsum('lts,lmvsc->lmvtc', kernel, shaped, precision=highest).reshape(MODES, MODES, FIELDS, 2)
    synthesised = jnp.einsum('lmj,lmfc->fcjm', legendre, bent_coef, precision=highest)
    combined = lax.complex(synthesised[:, 0], synthesised[:, 1])
    combined = jnp.pad(combined, ((0, 0), (0, 0), (0, NLON // 2 + 1 - MODES)))
    normal = (jnp.fft.irfft(combined, n=NLON, axis=-1) * NLON).reshape(VARS, INST, NLAT, NLON)
    ghost_layer = flow_state[:, :, RAD - 1] + normal
    sine_lat = jnp.sin(colatitude)[:, None]

    def one_layer(layer_index):
        centre = lax.dynamic_index_in_dim(flow_state, layer_index, 2, keepdims=False)
        below_layer = lax.dynamic_index_in_dim(flow_state, jnp.maximum(layer_index - 1, 0), 2, keepdims=False)
        above_layer = lax.dynamic_index_in_dim(flow_state, jnp.minimum(layer_index + 1, RAD - 1), 2, keepdims=False)
        inner_layer = jnp.where(layer_index > 0, below_layer, 0.0)
        outer_layer = jnp.where(layer_index < RAD - 1, above_layer, ghost_layer)
        zero_row = jnp.zeros_like(centre[:, :, :1])
        north_row = jnp.concatenate([zero_row, centre[:, :, :-1]], axis=2)
        south_row = jnp.concatenate([centre[:, :, 1:], zero_row], axis=2)
        west_col = jnp.roll(centre, 1, axis=3)
        east_col = jnp.roll(centre, -1, axis=3)
        return layer_residual(centre, inner_layer, outer_layer, north_row, south_row, west_col, east_col, sine_lat, jacobian_lat, jacobian_lon, jacobian_rad)
    layers = lax.map(one_layer, jnp.arange(RAD, dtype=jnp.int32))
    return (jnp.moveaxis(layers, 0, 2), normal)
```

```python
import functools
import math

import jax
import jax.numpy as jnp
import ml_dtypes
import numpy as np
from jax import lax
from jax.experimental import pallas as pl
from jax.experimental.pallas import tpu as pltpu
from jax.sharding import PartitionSpec as P

VARS, INST, RAD, NLAT, NLON, MODES = 5, 9, 4, 512, 2048, 256
FIELDS = VARS * INST
ROWS = 48
LATS, LONS = 32, 16
MESH = pl.DeviceIdType.MESH
f32, bf16 = jnp.float32, jnp.bfloat16
start_floor = -36.0


def split_table(table):
    high = table.astype(ml_dtypes.bfloat16)
    low = (table - high.astype(np.float64)).astype(ml_dtypes.bfloat16)
    return high, low


def circle_table():
    k = np.arange(128)
    table = np.zeros((LONS, 8, 3, 2, 128))
    for p in range(LONS):
        up = 2 * np.pi * p * k / 128
        down = -2 * np.pi * (p + 1) * k / 128
        rows = np.array(
            [
                [np.cos(up), np.sin(up)],
                [-np.sin(up), np.cos(up)],
                [np.cos(down), np.sin(down)],
                [np.sin(down), -np.cos(down)],
            ]
        )
        table[p, 0:4, 0] = rows
        table[p, 4:8, 1] = rows
        half = 2 * np.pi * (16 * p + 8) * k / 2048
        table[p, 4, 2, 0] = np.cos(up)
        table[p, 5, 2, 0] = -np.sin(up)
        table[p, 6, 2, 1] = np.cos(half)
        table[p, 7, 2, 1] = -np.sin(half)
    return table.reshape(LONS * 8, 768)


def twiddle_table():
    r = np.arange(8)[:, None]
    angle = 2 * np.pi * r * np.arange(128)[None] / 2048
    return np.concatenate([np.cos(angle), np.sin(angle)])


def time_tables():
    basis = np.zeros((9, 9))
    swapped = np.zeros((9, 9))
    s = np.arange(9)
    basis[:, 0] = 1
    for n in range(1, 5):
        c, d = np.cos(2 * np.pi * n * s / 9), np.sin(2 * np.pi * n * s / 9)
        basis[:, 2 * n - 1], basis[:, 2 * n] = c, d
        swapped[:, 2 * n - 1], swapped[:, 2 * n] = d, c
    eye = np.eye(VARS)
    both = np.zeros((45, 128))
    both[:, 0:45] = np.kron(eye, basis)
    both[:, 64:109] = np.kron(eye, swapped)
    into = np.zeros((256, 128))
    into[0:45] = both
    into[192:237] = both
    back = np.zeros((128, 128))
    for a in (0, 64):
        for b in (0, 64):
            back[a : a + 45, b : b + 45] = np.kron(eye, basis.T)
    return into, back


def ratio_rows():
    rows = np.zeros((16, 128))
    for v in range(VARS):
        rows[0, 9 * v] = 1 / 9
        for n in range(1, 5):
            rows[n, 9 * v + 2 * n - 1] = rows[n, 9 * v + 2 * n] = 2 / 9
            rows[4 + n, 64 + 9 * v + 2 * n - 1] = 2 / 9
            rows[4 + n, 64 + 9 * v + 2 * n] = -2 / 9
    return rows


def latitude_rows():
    column = np.arange(256)
    j = np.stack([16 * (column // 8) + 8 * h + column % 8 for h in (0, 1)])
    angle = (j.reshape(4, 128) + 0.5) * np.pi / NLAT
    angle = np.concatenate([angle, angle])
    return np.concatenate([np.cos(angle), np.sin(angle)])


def start_logs():
    return np.array(
        [
            0.5
            * (
                math.log((2 * m + 1) / (4 * math.pi))
                + math.lgamma(m + 0.5)
                - math.lgamma(m + 1.0)
                - 0.5 * math.log(math.pi)
            )
            for m in range(MODES)
        ]
    )


SPECTRAL = [0.5 * (-1) ** lag / math.sin(math.pi * lag / 9) for lag in range(1, 5)]


def split(value):
    high = value.astype(bf16)
    return high, (value - high.astype(f32)).astype(bf16)


def dot3(a, b):
    dot = functools.partial(jnp.dot, preferred_element_type=f32)
    return dot(a[0], b[0]) + (dot(a[0], b[1]) + dot(a[1], b[0]))


def weigh(terms):
    total = None
    for factor, value in terms:
        if abs(factor) < 1e-9:
            continue
        if abs(factor - 1) < 1e-9:
            total = value if total is None else total + value
        elif abs(factor + 1) < 1e-9:
            total = -value if total is None else total - value
        else:
            total = factor * value if total is None else total + factor * value
    return total


def sixteen(first, eighth, even, odd):
    cos = lambda n: math.cos(math.pi * n / 8)
    sin = lambda n: math.sin(math.pi * n / 8)
    plus, minus = first + eighth, first - eighth
    even_p = {d: even[d] + even[8 - d] for d in (1, 2, 3)}
    even_m = {d: even[d] - even[8 - d] for d in (1, 2, 3)}
    odd_p = {d: odd[d] + odd[8 - d] for d in (1, 2, 3)}
    odd_m = {d: odd[d] - odd[8 - d] for d in (1, 2, 3)}
    c, s = {}, {}
    for r in range(9):
        if r % 2 == 0:
            c[r] = weigh(
                [(1, plus), (cos(4 * r), even[4])] + [(cos(r * d), even_p[d]) for d in even_p]
            )
        else:
            c[r] = weigh([(1, minus)] + [(cos(r * d), even_m[d]) for d in even_m])
    for r in range(1, 8):
        if r % 2 == 0:
            s[r] = weigh([(sin(r * d), odd_m[d]) for d in odd_m])
        else:
            s[r] = weigh([(sin(4 * r), odd[4])] + [(sin(r * d), odd_p[d]) for d in odd_p])
    return c, s


def exchange(axis, me, count, send, recv, send_sem, recv_sem):
    def one(step, carry):
        peer = lax.rem(me + step, count)
        pltpu.make_async_remote_copy(
            src_ref=send.at[peer],
            dst_ref=recv.at[me],
            send_sem=send_sem,
            recv_sem=recv_sem,
            device_id={axis: peer},
            device_id_type=MESH,
        ).start()
        return carry

    lax.fori_loop(1, count, one, 0)


def drain(buffer, count, sem):
    part = buffer.at[pl.ds(0, count - 1)]
    pltpu.make_async_copy(part, part, sem).wait()


def far_field(
    x_hbm, jlat, jlon, jrad, cut, logs, real, imag,
    fwd_h, fwd_l, inv_h, inv_l, into_h, into_l, back_h, back_l, small_hbm,
    base_hbm, normal_hbm,
    shell, xv, base, s1, r1, s2, r2, s3, r3, s4, r4, s5, r5, s6, r6,
    row_send, row_recv, col_send, col_recv,
    circles, lines, raw, t_h, t_l, tt_h, tt_l, grow, drop, seed, mult,
    fwd_hv, fwd_lv, inv_hv, inv_lv, into_hv, into_lv, back_hv, back_lv, small,
    send_sem, recv_sem, halo_send, halo_recv, local,
):
    b = lax.axis_index("lat")
    p = lax.axis_index("lon")

    get_shell = pltpu.make_async_copy(x_hbm.at[:, 3], shell.at[pl.ds(0, FIELDS)], local.at[0])
    get_all = pltpu.make_async_copy(x_hbm, xv, local.at[1])
    get_shell.start()
    get_all.start()
    pairs = [
        (small_hbm, small), (fwd_h, fwd_hv), (fwd_l, fwd_lv), (inv_h, inv_hv), (inv_l, inv_lv),
        (into_h, into_hv), (into_l, into_lv), (back_h, back_hv), (back_l, back_lv),
    ]
    tables = [
        pltpu.make_async_copy(src, dst, local.at[2 + i]) for i, (src, dst) in enumerate(pairs)
    ]
    for copy in tables:
        copy.start()

    barrier = pltpu.get_barrier_semaphore()

    def greet(axis, me, count):
        def one(step, carry):
            pl.semaphore_signal(
                barrier, inc=1, device_id={axis: lax.rem(me + step, count)}, device_id_type=MESH
            )
            return carry

        lax.fori_loop(1, count, one, 0)

    greet("lon", p, LONS)
    greet("lat", b, LATS)

    shell[pl.ds(FIELDS, ROWS - FIELDS)] = jnp.zeros((ROWS - FIELDS, 16, 128), f32)
    get_shell.wait()
    shell_rows = shell.reshape(ROWS * 16, 128)
    for j in range(16):
        s1[j] = shell_rows[pl.ds(j, ROWS, stride=16), :]
    r1[p] = s1[p]
    pl.semaphore_wait(barrier, LONS + LATS - 2)
    exchange("lon", p, LONS, s1, r1, send_sem.at[0], recv_sem.at[0])

    get_all.wait()
    lane = lax.broadcasted_iota(jnp.int32, (16, 128), 1)
    row = lax.broadcasted_iota(jnp.int32, (16, 128), 0)
    x_rows = xv.reshape(FIELDS * RAD * 16, 128)
    row_send[0] = x_rows[pl.ds(0, 180, stride=16), :]
    row_send[1] = x_rows[pl.ds(15, 180, stride=16), :]

    def halo(axis, peer, index, send, recv):
        return pltpu.make_async_remote_copy(
            src_ref=send,
            dst_ref=recv,
            send_sem=halo_send.at[index],
            recv_sem=halo_recv.at[index],
            device_id={axis: peer},
            device_id_type=MESH,
        )

    halos = [
        halo("lat", lax.rem(b + LATS - 1, LATS), 0, row_send.at[0], row_recv.at[0]),
        halo("lat", lax.rem(b + 1, LATS), 1, row_send.at[1], row_recv.at[1]),
        halo("lon", lax.rem(p + LONS - 1, LONS), 2, col_send.at[0], col_recv.at[0]),
        halo("lon", lax.rem(p + 1, LONS), 3, col_send.at[1], col_recv.at[1]),
    ]
    halos[0].start()
    halos[1].start()

    def pack(f, packed):
        packed = list(packed)
        for r in range(RAD):
            x = xv[f, r]
            at = f + 64 * (r % 2)
            here = lane == at
            for side in (0, 1):
                i = 2 * side + r // 2
                packed[i] = jnp.where(here, pltpu.roll(x, lax.rem(at + side, 128), 1), packed[i])
        return tuple(packed)

    packed = lax.fori_loop(0, FIELDS, pack, (jnp.zeros((16, 128), f32),) * 4)
    for i in range(4):
        col_send[i // 2, i % 2] = packed[i]
    halos[2].start()
    halos[3].start()

    rho, g = b // 4, b % 4
    r = jnp.where(rho < 4, 2 * g + 1, 2 * g + 2)
    m = jnp.where(rho % 4 < 2, 16 * p + r, 16 * p + 16 - r)
    m = jnp.where((g == 3) & (rho >= 4), 16 * p + 8 * ((rho - 4) // 2), m)
    tables[0].wait()
    degree = lax.broadcasted_iota(jnp.int32, (MODES, 128), 0)
    deg = degree.astype(f32)
    order = m.astype(f32)
    order2 = order * order

    def factor(d):
        return jnp.sqrt(
            jnp.maximum(4.0 * d * d - 1.0, 1.0) / jnp.maximum(d * d - order2, 1.0)
        )

    factor_now, factor_prev = factor(deg), factor(deg - 1.0)
    grow[...] = jnp.where(degree > m, factor_now, 0.0)
    drop[...] = jnp.where(degree > m + 1, factor_now / factor_prev, 0.0)
    seed[...] = jnp.where(degree == m, 1.0, 0.0)
    cosine, sine_all = small[0:8], small[8:16]
    log_diagonal = logs[m] + order * jnp.log(sine_all)
    diagonal = jnp.where(
        log_diagonal >= start_floor, jnp.exp(jnp.maximum(log_diagonal, start_floor)), 0.0
    )

    def advance(i, state):
        latest, before = state
        first = pl.multiple_of(i * 8, 8)
        a8, q8, d8 = grow[pl.ds(first, 8)], drop[pl.ds(first, 8)], seed[pl.ds(first, 8)]
        for n in range(8):
            step = a8[n : n + 1] * cosine
            rest = d8[n : n + 1] * diagonal - q8[n : n + 1] * before
            latest, before = step * latest + rest, latest
            raw[pl.ds(pl.multiple_of((first + n) * 8, 8), 8)] = latest
        return latest, before

    zero = jnp.zeros((8, 128), f32)
    lax.fori_loop(0, MODES // 8, advance, (zero, zero))
    for s in range(4):
        h, half = s // 2, s % 2
        block = raw[pl.ds(s, MODES, stride=8), :]
        high, low = split(block)
        t_h[pl.ds(h * 256, 256), pl.ds(half * 128, 128)] = high
        t_l[pl.ds(h * 256, 256), pl.ds(half * 128, 128)] = low
        high, low = split(block.T)
        tt_h[pl.ds(half * 128, 128), pl.ds(h * 256, 256)] = high
        tt_l[pl.ds(half * 128, 128), pl.ds(h * 256, 256)] = low

    factors = jnp.zeros((MODES, 128), f32)
    for n in range(5):
        kept = jnp.where(degree <= cut[n], real[:, n : n + 1], 0.0)
        factors = factors + kept * small[32 + n : 33 + n]
        if n:
            kept = jnp.where(degree <= cut[n], imag[:, n - 1 : n], 0.0)
            factors = factors + kept * small[36 + n : 37 + n]
    mult[...] = factors * jnp.where(m == 0, 1.0, 2.0)

    j_own = 16 * b + p
    term = (
        lax.broadcasted_iota(jnp.int32, (8, 128), 0) * 128
        + lax.broadcasted_iota(jnp.int32, (8, 128), 1)
        + 1
    )
    angle = ((term * (2 * j_own + 1)) & (2 * NLAT - 1)).astype(f32) * (math.pi / NLAT)
    termf = term.astype(f32)
    part = jnp.where(term <= NLAT // 2, jnp.cos(angle) / (4.0 * termf * termf - 1.0), 0.0)
    series = jnp.sum(jnp.sum(part, axis=1, keepdims=True), axis=0, keepdims=True)
    weight = (2.0 / NLAT) * (1.0 - 2.0 * series) * (2.0 * math.pi / NLON)

    for i in (2, 3, 0, 1):
        halos[i].wait_recv()
    band = (16 * b + row).astype(f32)
    sine = jnp.sin((band + 0.5) * (math.pi / NLAT))
    half_sine = 0.5 * sine
    south_keep = jnp.where(b == LATS - 1, 0.0, 1.0)
    north_keep = jnp.where(b == 0, 0.0, 1.0)
    jl = [[jlat[v, w] for w in range(VARS)] for v in range(VARS)]
    jo = [[jlon[v, w] for w in range(VARS)] for v in range(VARS)]
    jr = [[jrad[v, w] for w in range(VARS)] for v in range(VARS)]

    def one_instance(t, carry):
        for r in range(RAD):
            lat_d, rad_d, lon_d, rest = [], [], [], []
            for w in range(VARS):
                f = w * INST + t
                x = xv[f, r]
                index = f * RAD + r
                at = f + 64 * (r % 2)
                south_row = row_recv[0, pl.ds(index, 1)] * south_keep
                north_row = row_recv[1, pl.ds(index, 1)] * north_keep
                south = jnp.where(row == 15, south_row, pltpu.roll(x, 15, 0))
                north = jnp.where(row == 0, north_row, pltpu.roll(x, 1, 0))
                east_col = pltpu.roll(col_recv[0, r // 2], 127 - at, 1)
                west_col = pltpu.roll(col_recv[1, r // 2], lax.rem(128 - at, 128), 1)
                east = jnp.where(lane == 127, east_col, pltpu.roll(x, 127, 1))
                west = jnp.where(lane == 0, west_col, pltpu.roll(x, 1, 1))
                above = xv[f, r + 1] if r < RAD - 1 else x
                below = xv[f, r - 1] if r > 0 else jnp.zeros_like(x)
                lat_d.append(half_sine * (south - north))
                rad_d.append(half_sine * (above - below))
                lon_d.append(0.5 * (east - west))
                spread = half_sine * (south + north + above + below - 4.0 * x)
                timing = -spread - 0.5 * (east + west - 2.0 * x)
                for lag in range(1, 5):
                    back = xv[w * INST + lax.rem(t + 9 - lag, 9), r]
                    ahead = xv[w * INST + lax.rem(t + lag, 9), r]
                    timing = timing + SPECTRAL[lag - 1] * (back - ahead)
                rest.append(timing)
            for v in range(VARS):
                total = rest[v]
                for w in range(VARS):
                    total = total + (
                        jl[v][w] * lat_d[w] + jr[v][w] * rad_d[w] + jo[v][w] * lon_d[w]
                    )
                base[v * INST + t, r] = total
        return carry

    lax.fori_loop(0, INST, one_instance, 0)
    put_base = pltpu.make_async_copy(base, base_hbm, local.at[0])
    put_base.start()

    for g4 in range(4):
        circles[pl.ds(64 * g4 + ROWS, 64 - ROWS)] = jnp.zeros((64 - ROWS, 768), f32)
    circles[pl.ds(0, 192), pl.ds(512, 256)] = jnp.zeros((192, 256), f32)
    circles[pl.ds(192, 64), pl.ds(256, 256)] = jnp.zeros((64, 256), f32)
    tw = lambda r: (small[16 + r : 17 + r], small[24 + r : 25 + r])
    for copy in tables[1:]:
        copy.wait()
    drain(r1, LONS, recv_sem.at[0])

    def analyse(i, carry):
        first = pl.multiple_of(i * 8, 8)
        x = [r1[d, pl.ds(first, 8)] for d in range(16)]
        even = {d: x[d] + x[16 - d] for d in range(1, 8)}
        odd = {d: x[d] - x[16 - d] for d in range(1, 8)}
        c, s = sixteen(x[0], x[8], even, odd)
        for r in range(1, 8):
            co, si = tw(r)
            at = pl.ds(64 * ((r - 1) // 2) + first, 8)
            column = 256 * ((r - 1) % 2)
            circles[at, pl.ds(column, 128)] = c[r] * co - s[r] * si
            circles[at, pl.ds(column + 128, 128)] = -s[r] * co - c[r] * si
        at = pl.ds(192 + first, 8)
        circles[at, pl.ds(512, 128)] = c[0]
        circles[at, pl.ds(640, 128)] = c[8]
        return carry

    lax.fori_loop(0, ROWS // 8, analyse, 0)
    found = dot3(split(circles[...]), (fwd_hv[...], fwd_lv[...])) * weight
    for half in (0, 1):
        s2[:, pl.ds(8 * half, 8), :] = found[128 * half : 128 * half + 128].T.reshape(16, 8, 128)
    r2[p] = s2[p]
    exchange("lon", p, LONS, s2, r2, send_sem.at[1], recv_sem.at[1])

    low_half = lax.broadcasted_iota(jnp.int32, (8, 128), 1) < 64
    drain(r2, LONS, recv_sem.at[1])
    r2_rows = r2.reshape(256, 128)
    for rho8 in range(8):
        for half in (0, 1):
            north8 = r2_rows[pl.ds(8 * half + rho8, 8, stride=16), :]
            south8 = r2_rows[pl.ds(128 + 8 * half + rho8, 8, stride=16), :]
            s3[4 * rho8 + 2 * half] = jnp.where(low_half, north8, pltpu.roll(south8, 64, 1))
            s3[4 * rho8 + 2 * half + 1] = jnp.where(low_half, pltpu.roll(north8, 64, 1), south8)
    r3[b] = s3[b]
    exchange("lat", b, LATS, s3, r3, send_sem.at[2], recv_sem.at[2])
    drain(r3, LATS, recv_sem.at[2])

    degrees = dot3((t_h[...], t_l[...]), split(r3[...].reshape(256, 128)))
    degrees = jnp.concatenate([degrees[0:256], degrees[256:512]], axis=1)
    modes = dot3(split(degrees), (into_hv[...], into_lv[...])) * mult[...]
    bent = dot3(split(modes), (back_hv[...], back_lv[...]))
    left = lax.broadcasted_iota(jnp.int32, (MODES, 128), 1) < 64
    bent = jnp.concatenate([jnp.where(left, bent, 0.0), jnp.where(left, 0.0, bent)], axis=0)
    s4[...] = dot3((tt_h[...], tt_l[...]), split(bent)).reshape(32, 8, 128)
    r4[b] = s4[b]
    exchange("lat", b, LATS, s4, r4, send_sem.at[3], recv_sem.at[3])
    drain(r4, LATS, recv_sem.at[3])

    s5_rows = s5.reshape(256, 128)
    for rho8 in range(8):
        for half in (0, 1):
            one, two = r4[4 * rho8 + 2 * half], r4[4 * rho8 + 2 * half + 1]
            s5_rows[pl.ds(8 * half + rho8, 8, stride=16), :] = jnp.where(
                low_half, one, pltpu.roll(two, 64, 1)
            )
            s5_rows[pl.ds(128 + 8 * half + rho8, 8, stride=16), :] = jnp.where(
                low_half, pltpu.roll(one, 64, 1), two
            )
    r5[p] = s5[p]
    exchange("lon", p, LONS, s5, r5, send_sem.at[4], recv_sem.at[4])
    drain(r5, LONS, recv_sem.at[4])

    found = jnp.concatenate(
        [r5[:, pl.ds(8 * half, 8), :].reshape(128, 128).T for half in (0, 1)], axis=0
    )
    lines[...] = dot3(split(found), (inv_hv[...], inv_lv[...]))

    def synthesise(i, carry):
        first = pl.multiple_of(i * 8, 8)
        even, odd = {}, {}
        for r in range(1, 8):
            co, si = tw(r)
            at = pl.ds(64 * ((r - 1) // 2) + first, 8)
            column = 256 * ((r - 1) % 2)
            re, im = lines[at, pl.ds(column, 128)], lines[at, pl.ds(column + 128, 128)]
            even[r] = re * co - im * si
            odd[r] = re * si + im * co
        at = pl.ds(192 + first, 8)
        c, s = sixteen(lines[at, pl.ds(512, 128)], lines[at, pl.ds(640, 128)], even, odd)
        s6[0, pl.ds(first, 8)] = c[0]
        s6[8, pl.ds(first, 8)] = c[8]
        for d in range(1, 8):
            s6[d, pl.ds(first, 8)] = c[d] - s[d]
            s6[16 - d, pl.ds(first, 8)] = c[d] + s[d]
        return carry

    lax.fori_loop(0, ROWS // 8, synthesise, 0)
    r6[p] = s6[p]
    exchange("lon", p, LONS, s6, r6, send_sem.at[5], recv_sem.at[5])
    drain(r6, LONS, recv_sem.at[5])
    put_normal = pltpu.make_async_copy(r6, normal_hbm, local.at[1])
    put_normal.start()
    for i, (buffer, count) in enumerate(
        [(s1, LONS), (s2, LONS), (s3, LATS), (s4, LATS), (s5, LONS), (s6, LONS)]
    ):
        drain(buffer, count, send_sem.at[i])
    for copy in halos:
        copy.wait_send()
    put_base.wait()
    put_normal.wait()


def finish(base_hbm, circles, jrad, out_hbm, normal, layer, sem):
    b = lax.axis_index("lat")
    inner = pltpu.make_async_copy(
        base_hbm.at[:, pl.ds(0, 3)], out_hbm.at[:, pl.ds(0, 3)], sem.at[0]
    )
    inner.start()
    get = pltpu.make_async_copy(base_hbm.at[:, 3], layer, sem.at[1])
    get.start()
    row = lax.broadcasted_iota(jnp.int32, (16, 128), 0)
    half_sine = 0.5 * jnp.sin(((16 * b + row).astype(f32) + 0.5) * (math.pi / NLAT))
    jr = [[jrad[v, w] for w in range(VARS)] for v in range(VARS)]
    rows = circles.reshape(16 * ROWS, 128)
    get.wait()

    def one_instance(t, carry):
        n = []
        for w in range(VARS):
            value = rows[pl.ds(w * INST + t, 16, stride=ROWS), :]
            normal[w * INST + t] = value
            n.append(value)
        for v in range(VARS):
            total = -n[v]
            for w in range(VARS):
                total = total + jr[v][w] * n[w]
            layer[v * INST + t] = layer[v * INST + t] + half_sine * total
        return carry

    lax.fori_loop(0, INST, one_instance, 0)
    put = pltpu.make_async_copy(layer, out_hbm.at[:, 3], sem.at[1])
    put.start()
    put.wait()
    inner.wait()


def shards(flow_state, jacobian_lat, jacobian_lon, jacobian_rad, ratio_real, ratio_imag, cut):
    x = flow_state.reshape(FIELDS, RAD, 16, 128)
    table = circle_table()
    into, back = time_tables()
    small = np.zeros((48, 128), np.float32)
    small[0:16] = latitude_rows()
    small[16:32] = twiddle_table()
    small[32:48] = ratio_rows()
    logs = start_logs().astype(np.float32)
    constants = [
        jnp.asarray(part)
        for full in (table.T, table, into, back)
        for part in split_table(np.ascontiguousarray(full))
    ] + [jnp.asarray(small)]
    smem = pl.BlockSpec(memory_space=pltpu.SMEM)
    vmem = pl.BlockSpec(memory_space=pltpu.VMEM)
    hbm = pl.BlockSpec(memory_space=pl.ANY)
    v = lambda *shape: pltpu.VMEM(shape, f32)
    w = lambda *shape: pltpu.VMEM(shape, bf16)
    base, circles = pl.pallas_call(
        far_field,
        out_shape=[
            jax.ShapeDtypeStruct((FIELDS, RAD, 16, 128), f32),
            jax.ShapeDtypeStruct((16, ROWS, 128), f32),
        ],
        in_specs=[hbm] + [smem] * 5 + [vmem] * 2 + [hbm] * len(constants),
        out_specs=[hbm, hbm],
        scratch_shapes=[
            v(ROWS, 16, 128), v(FIELDS, RAD, 16, 128), v(FIELDS, RAD, 16, 128),
            v(16, ROWS, 128), v(16, ROWS, 128),
            v(16, 16, 128), v(16, 16, 128),
            v(32, 8, 128), v(32, 8, 128),
            v(32, 8, 128), v(32, 8, 128),
            v(16, 16, 128), v(16, 16, 128),
            v(16, ROWS, 128), v(16, ROWS, 128),
            v(2, 180, 128), v(2, 180, 128), v(2, 2, 16, 128), v(2, 2, 16, 128),
            v(256, 768), v(256, 768), v(MODES * 8, 128),
            w(512, 256), w(512, 256), w(256, 512), w(256, 512),
            v(MODES, 128), v(MODES, 128), v(MODES, 128), v(MODES, 128),
            w(768, 128), w(768, 128), w(128, 768), w(128, 768),
            w(256, 128), w(256, 128), w(128, 128), w(128, 128), v(48, 128),
            pltpu.SemaphoreType.DMA((6,)), pltpu.SemaphoreType.DMA((6,)),
            pltpu.SemaphoreType.DMA((4,)), pltpu.SemaphoreType.DMA((4,)),
            pltpu.SemaphoreType.DMA((11,)),
        ],
        compiler_params=pltpu.CompilerParams(
            collective_id=0, has_side_effects=True, vmem_limit_bytes=40 * 1024 * 1024
        ),
        name="far_field",
    )(x, jacobian_lat, jacobian_lon, jacobian_rad, cut, jnp.asarray(logs), ratio_real, ratio_imag,
      *constants)
    residual, normal = pl.pallas_call(
        finish,
        out_shape=[
            jax.ShapeDtypeStruct((FIELDS, RAD, 16, 128), f32),
            jax.ShapeDtypeStruct((FIELDS, 16, 128), f32),
        ],
        in_specs=[hbm, vmem, smem],
        out_specs=[hbm, vmem],
        scratch_shapes=[v(FIELDS, 16, 128), pltpu.SemaphoreType.DMA((2,))],
        compiler_params=pltpu.CompilerParams(vmem_limit_bytes=16 * 1024 * 1024),
        name="finish",
    )(base, circles, jacobian_rad)
    return (
        residual.reshape(VARS, INST, RAD, 16, 128),
        normal.reshape(VARS, INST, 16, 128),
    )


def solution(mesh):
    placed = (P(None, None, None, "lat", "lon"), P(), P(), P(), P(), P(), P())
    return jax.shard_map(
        shards,
        mesh=mesh,
        in_specs=placed,
        out_specs=(P(None, None, None, "lat", "lon"), P(None, None, "lat", "lon")),
        check_vma=False,
    )
```

```python
import functools
import math

import jax
import jax.numpy as jnp
import ml_dtypes
import numpy as np
from jax import lax
from jax.experimental import pallas as pl
from jax.experimental.pallas import tpu as pltpu
from jax.sharding import PartitionSpec as P

VARS, INST, RAD, NLAT, NLON, MODES = 5, 9, 4, 512, 2048, 256
FIELDS = VARS * INST
ROWS = 48
LATS, LONS = 32, 16
MESH = pl.DeviceIdType.MESH
f32, bf16 = jnp.float32, jnp.bfloat16
start_floor = -36.0


def split_table(table):
    high = table.astype(ml_dtypes.bfloat16)
    low = (table - high.astype(np.float64)).astype(ml_dtypes.bfloat16)
    return high, low


def circle_table():
    k = np.arange(128)
    table = np.zeros((LONS, 8, 3, 2, 128))
    for p in range(LONS):
        up = 2 * np.pi * p * k / 128
        down = -2 * np.pi * (p + 1) * k / 128
        rows = np.array(
            [
                [np.cos(up), np.sin(up)],
                [-np.sin(up), np.cos(up)],
                [np.cos(down), np.sin(down)],
                [np.sin(down), -np.cos(down)],
            ]
        )
        table[p, 0:4, 0] = rows
        table[p, 4:8, 1] = rows
        half = 2 * np.pi * (16 * p + 8) * k / 2048
        table[p, 4, 2, 0] = np.cos(up)
        table[p, 5, 2, 0] = -np.sin(up)
        table[p, 6, 2, 1] = np.cos(half)
        table[p, 7, 2, 1] = -np.sin(half)
    return table.reshape(LONS * 8, 768)


def twiddle_table():
    r = np.arange(8)[:, None]
    angle = 2 * np.pi * r * np.arange(128)[None] / 2048
    return np.concatenate([np.cos(angle), np.sin(angle)])


def slot_table():
    pairs = [[(v, n, 0), (v, n, 1)] for v in range(VARS) for n in range(1, 5)]
    pairs += [[(0, 0, 0), (1, 0, 0)], [(2, 0, 0), (3, 0, 0)], [(4, 0, 0), None], [None, None]]
    return [sum(pairs[3 * z : 3 * z + 3], []) for z in range(8)]


SLOTS = slot_table()
PLACE = {item: (z, i) for z in range(8) for i, item in enumerate(SLOTS[z]) if item}


def ratio_rows():
    rows = np.zeros((8, 16, 2, 8, 8))
    for z in range(8):
        for i, item in enumerate(SLOTS[z]):
            if item is None:
                continue
            _, n, part = item
            rows[z, n, :, i] = 2 / 9 if n else 1 / 9
            if n:
                rows[z, 7 + n, :, i] = -2 / 9 if part else 2 / 9
    return rows.reshape(8, 16, 128)


def fold_time(first, even, odd):
    c, s = {}, {}
    for n in range(1, 5):
        angles = {k: 2 * math.pi * n * k / 9 for k in range(1, 5)}
        c[n] = weigh([(1, first)] + [(math.cos(angles[k]), even[k]) for k in angles])
        s[n] = weigh([(math.sin(angles[k]), odd[k]) for k in angles])
    return c, s


def latitude_rows():
    column = np.arange(256)
    j = np.stack([16 * (column // 8) + 8 * h + column % 8 for h in (0, 1)])
    angle = (j.reshape(4, 128) + 0.5) * np.pi / NLAT
    angle = np.concatenate([angle, angle])
    return np.concatenate([np.cos(angle), np.sin(angle)])


def start_logs():
    return np.array(
        [
            0.5
            * (
                math.log((2 * m + 1) / (4 * math.pi))
                + math.lgamma(m + 0.5)
                - math.lgamma(m + 1.0)
                - 0.5 * math.log(math.pi)
            )
            for m in range(MODES)
        ]
    )


SPECTRAL = [0.5 * (-1) ** lag / math.sin(math.pi * lag / 9) for lag in range(1, 5)]


def split(value):
    high = value.astype(bf16)
    return high, (value - high.astype(f32)).astype(bf16)


def dot(a, b):
    return jnp.dot(a, b, preferred_element_type=f32)


def dot_wide(a, wide):
    total = dot(a[0], wide)
    return total[:, 0:128] + (total[:, 128:256] + dot(a[1], wide[:, 0:128]))


def weigh(terms):
    total = None
    for factor, value in terms:
        if abs(factor) < 1e-9:
            continue
        if abs(factor - 1) < 1e-9:
            total = value if total is None else total + value
        elif abs(factor + 1) < 1e-9:
            total = -value if total is None else total - value
        else:
            total = factor * value if total is None else total + factor * value
    return total


def sixteen(first, eighth, even, odd):
    cos = lambda n: math.cos(math.pi * n / 8)
    sin = lambda n: math.sin(math.pi * n / 8)
    plus, minus = first + eighth, first - eighth
    even_p = {d: even[d] + even[8 - d] for d in (1, 2, 3)}
    even_m = {d: even[d] - even[8 - d] for d in (1, 2, 3)}
    odd_p = {d: odd[d] + odd[8 - d] for d in (1, 2, 3)}
    odd_m = {d: odd[d] - odd[8 - d] for d in (1, 2, 3)}
    c, s = {}, {}
    for r in range(9):
        if r % 2 == 0:
            c[r] = weigh(
                [(1, plus), (cos(4 * r), even[4])] + [(cos(r * d), even_p[d]) for d in even_p]
            )
        else:
            c[r] = weigh([(1, minus)] + [(cos(r * d), even_m[d]) for d in even_m])
    for r in range(1, 8):
        if r % 2 == 0:
            s[r] = weigh([(sin(r * d), odd_m[d]) for d in odd_m])
        else:
            s[r] = weigh([(sin(4 * r), odd[4])] + [(sin(r * d), odd_p[d]) for d in odd_p])
    return c, s


def exchange(axis, me, count, send, recv, send_sem, recv_sem):
    def one(step, carry):
        peer = lax.rem(me + step, count)
        pltpu.make_async_remote_copy(
            src_ref=send.at[peer],
            dst_ref=recv.at[me],
            send_sem=send_sem,
            recv_sem=recv_sem,
            device_id={axis: peer},
            device_id_type=MESH,
        ).start()
        return carry

    lax.fori_loop(1, count, one, 0)


def drain(buffer, count, sem):
    part = buffer.at[pl.ds(0, count - 1)]
    pltpu.make_async_copy(part, part, sem).wait()


def far_field(
    x_hbm, jlat_hbm, jlon_hbm, jrad_hbm, cut_hbm, real_hbm, imag_hbm, fwd_hbm, inv_hbm, small_hbm,
    select_hbm, base_hbm, normal_hbm,
    shell, xv, base, s1, r1, s2, r2, s3, r3, s4, r4, s5, r5, s6,
    row_send, row_recv, col_send, col_recv,
    circles, lines, raw, t_h, t_l, tt_h, tt_l, grow, drop, seed, mult,
    fwd, inv, small, select, jlat, jlon, jrad, cut, real, imag,
    send_sem, recv_sem, halo_send, halo_recv, local,
):
    b = lax.axis_index("lat")
    p = lax.axis_index("lon")
    z, x = p // 2, p % 2
    partner = p + 1 - 2 * x

    barrier = pltpu.get_barrier_semaphore()

    def greet(axis, me, count):
        def one(step, carry):
            pl.semaphore_signal(
                barrier, inc=1, device_id={axis: lax.rem(me + step, count)}, device_id_type=MESH
            )
            return carry

        lax.fori_loop(1, count, one, 0)

    greet("lon", p, LONS)
    greet("lat", b, LATS)

    get_shell = pltpu.make_async_copy(x_hbm.at[:, 3], shell, local.at[0])
    get_all = pltpu.make_async_copy(x_hbm, xv, local.at[1])
    get_shell.start()
    get_all.start()
    pairs = [
        (small_hbm, small), (real_hbm, real), (imag_hbm, imag), (cut_hbm, cut),
        (jlat_hbm, jlat), (jlon_hbm, jlon), (jrad_hbm, jrad),
        (select_hbm, select), (fwd_hbm, fwd), (inv_hbm, inv),
    ]
    tables = [
        pltpu.make_async_copy(src, dst, local.at[2 + i]) for i, (src, dst) in enumerate(pairs)
    ]
    for copy in tables:
        copy.start()

    get_shell.wait()
    for z8 in range(8):
        for i, item in enumerate(SLOTS[z8]):
            if item is None:
                for h in (0, 1):
                    s1[2 * z8 + h, pl.ds(8 * i, 8)] = jnp.zeros((8, 128), f32)
    for v in range(VARS):
        for h in (0, 1):
            q = [shell[v * INST + t, pl.ds(8 * h, 8)] for t in range(INST)]
            even = {k: q[k] + q[9 - k] for k in range(1, 5)}
            odd = {k: q[k] - q[9 - k] for k in range(1, 5)}
            c, s = fold_time(q[0], even, odd)
            parts = {(v, 0, 0): q[0] + sum(even.values())}
            for n in range(1, 5):
                parts[v, n, 0], parts[v, n, 1] = c[n], s[n]
            for item, value in parts.items():
                z8, i = PLACE[item]
                s1[2 * z8 + h, pl.ds(8 * i, 8)] = value
    r1[p] = s1[p]
    pl.semaphore_wait(barrier, LONS + LATS - 2)
    exchange("lon", p, LONS, s1, r1, send_sem.at[0], recv_sem.at[0])

    get_all.wait()
    lane = lax.broadcasted_iota(jnp.int32, (16, 128), 1)
    row = lax.broadcasted_iota(jnp.int32, (16, 128), 0)
    x_rows = xv.reshape(FIELDS * RAD * 16, 128)
    row_send[0] = x_rows[pl.ds(0, 180, stride=16), :]
    row_send[1] = x_rows[pl.ds(15, 180, stride=16), :]

    def halo(axis, peer, index, send, recv):
        return pltpu.make_async_remote_copy(
            src_ref=send,
            dst_ref=recv,
            send_sem=halo_send.at[index],
            recv_sem=halo_recv.at[index],
            device_id={axis: peer},
            device_id_type=MESH,
        )

    halos = [
        halo("lat", lax.rem(b + LATS - 1, LATS), 0, row_send.at[0], row_recv.at[0]),
        halo("lat", lax.rem(b + 1, LATS), 1, row_send.at[1], row_recv.at[1]),
        halo("lon", lax.rem(p + LONS - 1, LONS), 2, col_send.at[0], col_recv.at[0]),
        halo("lon", lax.rem(p + 1, LONS), 3, col_send.at[1], col_recv.at[1]),
    ]
    halos[0].start()
    halos[1].start()

    q_own, g = b // 2, 2 * (b % 2) + x
    orders = []
    for s in (0, 1):
        r = 2 * g + 1 + s
        for t in (0, 1):
            m = 16 * q_own + r if t == 0 else 16 * q_own + 16 - r
            if s == 1:
                m = jnp.where(g == 3, 16 * q_own + 8 * t, m)
            orders.append(m)
    for copy in tables[:8]:
        copy.wait()
    degree = lax.broadcasted_iota(jnp.int32, (MODES, 128), 0)
    deg = degree.astype(f32)
    cosine, sine_all = small[0:8], small[8:16]
    log_sine = jnp.log(sine_all)
    entry = lax.broadcasted_iota(jnp.int32, (2, 128), 0) * 128 + lax.broadcasted_iota(
        jnp.int32, (2, 128), 1
    )
    diagonals = []
    for mu, m in enumerate(orders):
        order = m.astype(f32)
        order2 = order * order

        def factor(d):
            return jnp.sqrt(
                jnp.maximum(4.0 * d * d - 1.0, 1.0) / jnp.maximum(d * d - order2, 1.0)
            )

        factor_now, factor_prev = factor(deg), factor(deg - 1.0)
        grow[mu] = jnp.where(degree > m, factor_now, 0.0)
        drop[mu] = jnp.where(degree > m + 1, factor_now / factor_prev, 0.0)
        seed[mu] = jnp.where(degree == m, 1.0, 0.0)
        log_start = jnp.where(entry == m, small[48:50], 0.0)
        log_start = jnp.sum(jnp.sum(log_start, axis=1, keepdims=True), axis=0, keepdims=True)
        log_diagonal = log_start + order * log_sine
        diagonals.append(
            jnp.where(
                log_diagonal >= start_floor, jnp.exp(jnp.maximum(log_diagonal, start_floor)), 0.0
            )
        )

    def advance(i, state):
        first = pl.multiple_of(i * 8, 8)
        at = pl.ds(first, 8)
        rows = [(grow[mu, at], drop[mu, at], seed[mu, at]) for mu in range(4)]
        state = list(state)
        for n in range(8):
            row_at = pl.ds(pl.multiple_of((first + n) * 8, 8), 8)
            for mu in range(4):
                a8, q8, d8 = rows[mu]
                latest, before = state[mu]
                step = a8[n : n + 1] * cosine
                rest = d8[n : n + 1] * diagonals[mu] - q8[n : n + 1] * before
                fresh = step * latest + rest
                raw[mu, row_at] = fresh
                state[mu] = (fresh, latest)
        return tuple(state)

    zero = jnp.zeros((8, 128), f32)
    lax.fori_loop(0, MODES // 8, advance, ((zero, zero),) * 4)
    for mu in range(4):
        for s in range(4):
            h, half = s // 2, s % 2
            block = raw[mu, pl.ds(s, MODES, stride=8), :]
            high, low = split(block)
            t_h[2 * mu + h, :, pl.ds(half * 128, 128)] = high
            t_l[2 * mu + h, :, pl.ds(half * 128, 128)] = low
            high, low = split(block.T)
            tt_h[2 * mu + h, pl.ds(half * 128, 128), :] = high
            tt_l[2 * mu + h, pl.ds(half * 128, 128), :] = low

    lane_all = lax.broadcasted_iota(jnp.int32, (MODES, 128), 1)
    mu_lane = (lane_all // 2) % 4
    own = [(mu_lane == mu) & (lane_all // 64 == h) for mu in range(4) for h in (0, 1)]
    own_low = [mask[0:256] for mask in own]

    def by_degree(ratios, first, rows):
        count = ratios.shape[0]
        frequency = lax.broadcasted_iota(jnp.int32, (count, MODES), 0) + first
        last = jnp.zeros((count, MODES), jnp.int32)
        for n in range(first, 5):
            last = jnp.where(frequency == n, cut[n], last)
        kept = lax.broadcasted_iota(jnp.int32, (count, MODES), 1) <= last
        return lax.dot_general(
            jnp.where(kept, ratios[...], 0.0),
            rows,
            (((0,), (0,)), ((), ())),
            precision=lax.Precision.HIGHEST,
            preferred_element_type=f32,
        )

    w_lane = jnp.full((MODES, 128), 2.0, f32)
    for mu, m in enumerate(orders):
        w_lane = jnp.where(mu_lane == mu, jnp.where(m == 0, 1.0, 2.0), w_lane)
    mult[0] = by_degree(real, 0, select[z, 0:5]) * w_lane
    mult[1] = by_degree(imag, 1, select[z, 8:12]) * w_lane

    j_own = 16 * b + 8 * x + lax.broadcasted_iota(jnp.int32, (8, 256), 0)
    term = lax.broadcasted_iota(jnp.int32, (8, 256), 1) + 1
    angle = ((term * (2 * j_own + 1)) & (2 * NLAT - 1)).astype(f32) * (math.pi / NLAT)
    termf = term.astype(f32)
    series = jnp.sum(jnp.cos(angle) / (4.0 * termf * termf - 1.0), axis=1, keepdims=True)
    weight = (2.0 / NLAT) * (1.0 - 2.0 * series) * (2.0 * math.pi / NLON)
    weight = jnp.broadcast_to(weight, (8, 128))

    for g4 in range(4):
        circles[pl.ds(64 * g4 + ROWS, 64 - ROWS)] = jnp.zeros((64 - ROWS, 768), f32)
    circles[pl.ds(0, 192), pl.ds(512, 256)] = jnp.zeros((192, 256), f32)
    circles[pl.ds(192, 64), pl.ds(256, 256)] = jnp.zeros((64, 256), f32)
    place = lambda g4: 2 * (g4 % 2) + g4 // 2
    tw = lambda r: (small[16 + r : 17 + r], small[24 + r : 25 + r])
    for copy in tables[8:]:
        copy.wait()
    drain(r1, LONS, recv_sem.at[0])

    def analyse(i, carry):
        first = pl.multiple_of(i * 8, 8)
        x = [r1[d, pl.ds(first, 8)] for d in range(16)]
        even = {d: x[d] + x[16 - d] for d in range(1, 8)}
        odd = {d: x[d] - x[16 - d] for d in range(1, 8)}
        c, s = sixteen(x[0], x[8], even, odd)
        for r in range(1, 8):
            co, si = tw(r)
            at = pl.ds(64 * place((r - 1) // 2) + first, 8)
            column = 256 * ((r - 1) % 2)
            circles[at, pl.ds(column, 128)] = c[r] * co - s[r] * si
            circles[at, pl.ds(column + 128, 128)] = -s[r] * co - c[r] * si
        at = pl.ds(192 + first, 8)
        circles[at, pl.ds(512, 128)] = c[0]
        circles[at, pl.ds(640, 128)] = c[8]
        return carry

    lax.fori_loop(0, ROWS // 8, analyse, 0)
    found = dot_wide(split(circles[...]), fwd[...])
    lane8 = lax.broadcasted_iota(jnp.int32, (8, 128), 1)
    low_half = lane8 < 64
    granule = [lane8 // 8 == i for i in range(16)]

    def turn(value, granules):
        return pltpu.roll(value, (8 * granules) % 128, 1) if granules % 16 else value

    for half in (0, 1):
        tiles = {}
        for g2 in (0, 1):
            for i in range(6):
                first = 64 * (2 * half + g2) + 8 * i
                tiles[8 * g2 + i] = found[first : first + 8] * weight
        for q in range(16):
            message = jnp.zeros((8, 128), f32)
            for i, tile in tiles.items():
                message = jnp.where(granule[i], turn(tile, i - q), message)
            s2[half, q] = message
    def pass_on(send, recv, index):
        return pltpu.make_async_remote_copy(
            src_ref=send.at[1 - x],
            dst_ref=recv.at[x],
            send_sem=send_sem.at[index],
            recv_sem=recv_sem.at[index],
            device_id={"lon": partner},
            device_id_type=MESH,
        )

    second = pass_on(s2, r2, 1)
    second.start()
    r2[x] = s2[x]
    second.wait_recv()
    for q in range(16):
        one, two = r2[0, q], r2[1, q]
        s3[2 * q] = jnp.where(low_half, one, pltpu.roll(two, 64, 1))
        s3[2 * q + 1] = jnp.where(low_half, pltpu.roll(one, 64, 1), two)
    r3[b] = s3[b]
    exchange("lat", b, LATS, s3, r3, send_sem.at[2], recv_sem.at[2])
    def pack(f, packed):
        packed = list(packed)
        for r in range(RAD):
            x = xv[f, r]
            at = f + 64 * (r % 2)
            here = lane == at
            for side in (0, 1):
                i = 2 * side + r // 2
                packed[i] = jnp.where(here, pltpu.roll(x, lax.rem(at + side, 128), 1), packed[i])
        return tuple(packed)

    packed = lax.fori_loop(0, FIELDS, pack, (jnp.zeros((16, 128), f32),) * 4)
    for i in range(4):
        col_send[i // 2, i % 2] = packed[i]
    halos[2].start()
    halos[3].start()

    drain(r3, LATS, recv_sem.at[2])

    wide = jnp.concatenate(split(r3[...].reshape(256, 128)), axis=1)
    degrees = jnp.zeros((MODES, 128), f32)
    for i in range(8):
        degrees = jnp.where(own[i], dot_wide((t_h[i], t_l[i]), wide), degrees)
    degrees = degrees + pltpu.roll(degrees, 64, 1)
    swapped = jnp.where(
        (lane_all // 8) % 2 == 0, pltpu.roll(degrees, 120, 1), pltpu.roll(degrees, 8, 1)
    )
    bent = mult[0] * degrees + mult[1] * swapped
    wide = jnp.concatenate(split(bent), axis=1)
    rows_out = jnp.zeros((256, 128), f32)
    for i in range(8):
        rows_out = jnp.where(own_low[i], dot_wide((tt_h[i], tt_l[i]), wide), rows_out)
    s4[...] = rows_out.reshape(32, 8, 128)
    r4[b] = s4[b]
    exchange("lat", b, LATS, s4, r4, send_sem.at[3], recv_sem.at[3])
    for i in (2, 3, 0, 1):
        halos[i].wait_recv()
    band = (16 * b + row).astype(f32)
    sine = jnp.sin((band + 0.5) * (math.pi / NLAT))
    half_sine = 0.5 * sine
    south_keep = jnp.where(b == LATS - 1, 0.0, 1.0)
    north_keep = jnp.where(b == 0, 0.0, 1.0)
    jl = [[jlat[v, w] for w in range(VARS)] for v in range(VARS)]
    jo = [[jlon[v, w] for w in range(VARS)] for v in range(VARS)]
    jr = [[jrad[v, w] for w in range(VARS)] for v in range(VARS)]

    def one_instance(t, carry):
        for r in range(RAD):
            lat_d, rad_d, lon_d, rest = [], [], [], []
            for w in range(VARS):
                f = w * INST + t
                x = xv[f, r]
                index = f * RAD + r
                at = f + 64 * (r % 2)
                south_row = row_recv[0, pl.ds(index, 1)] * south_keep
                north_row = row_recv[1, pl.ds(index, 1)] * north_keep
                south = jnp.where(row == 15, south_row, pltpu.roll(x, 15, 0))
                north = jnp.where(row == 0, north_row, pltpu.roll(x, 1, 0))
                east_col = pltpu.roll(col_recv[0, r // 2], 127 - at, 1)
                west_col = pltpu.roll(col_recv[1, r // 2], lax.rem(128 - at, 128), 1)
                east = jnp.where(lane == 127, east_col, pltpu.roll(x, 127, 1))
                west = jnp.where(lane == 0, west_col, pltpu.roll(x, 1, 1))
                above = xv[f, r + 1] if r < RAD - 1 else x
                below = xv[f, r - 1] if r > 0 else jnp.zeros_like(x)
                lat_d.append(half_sine * (south - north))
                rad_d.append(half_sine * (above - below))
                lon_d.append(0.5 * (east - west))
                spread = half_sine * (south + north + above + below - 4.0 * x)
                timing = -spread - 0.5 * (east + west - 2.0 * x)
                for lag in range(1, 5):
                    back = xv[w * INST + lax.rem(t + 9 - lag, 9), r]
                    ahead = xv[w * INST + lax.rem(t + lag, 9), r]
                    timing = timing + SPECTRAL[lag - 1] * (back - ahead)
                rest.append(timing)
            for v in range(VARS):
                total = rest[v]
                for w in range(VARS):
                    total = total + (
                        jl[v][w] * lat_d[w] + jr[v][w] * rad_d[w] + jo[v][w] * lon_d[w]
                    )
                base[v * INST + t, r] = total
        return carry

    lax.fori_loop(0, INST, one_instance, 0)
    put_base = pltpu.make_async_copy(base, base_hbm, local.at[0])
    put_base.start()

    drain(r4, LATS, recv_sem.at[3])

    for q in range(16):
        one, two = r4[2 * q], r4[2 * q + 1]
        s5[0, q] = jnp.where(low_half, one, pltpu.roll(two, 64, 1))
        s5[1, q] = jnp.where(low_half, pltpu.roll(one, 64, 1), two)
    fifth = pass_on(s5, r5, 4)
    fifth.start()
    r5[x] = s5[x]
    fifth.wait_recv()

    blocks = []
    for half in (0, 1):
        messages = [r5[half, q] for q in range(16)]
        for g2 in (0, 1):
            for i in range(6):
                tile = turn(messages[0], -(8 * g2 + i))
                for q in range(1, 16):
                    tile = jnp.where(granule[q], turn(messages[q], q - 8 * g2 - i), tile)
                blocks.append(tile)
            blocks.append(jnp.zeros((16, 128), f32))
    found = split(jnp.concatenate(blocks, axis=0))
    lines[...] = dot(jnp.concatenate(found, axis=1), inv[0:256]) + dot(found[0], inv[256:384])

    def synthesise(i, carry):
        first = pl.multiple_of(i * 8, 8)
        even, odd = {}, {}
        for r in range(1, 8):
            co, si = tw(r)
            at = pl.ds(64 * place((r - 1) // 2) + first, 8)
            column = 256 * ((r - 1) % 2)
            re, im = lines[at, pl.ds(column, 128)], lines[at, pl.ds(column + 128, 128)]
            even[r] = re * co - im * si
            odd[r] = re * si + im * co
        at = pl.ds(192 + first, 8)
        c, s = sixteen(lines[at, pl.ds(512, 128)], lines[at, pl.ds(640, 128)], even, odd)
        s6[0, pl.ds(first, 8)] = c[0]
        s6[8, pl.ds(first, 8)] = c[8]
        for d in range(1, 8):
            s6[d, pl.ds(first, 8)] = c[d] - s[d]
            s6[16 - d, pl.ds(first, 8)] = c[d] + s[d]
        return carry

    lax.fori_loop(0, ROWS // 8, synthesise, 0)
    keep = pltpu.make_async_copy(s6.at[p], normal_hbm.at[p], local.at[1])
    keep.start()
    exchange("lon", p, LONS, s6, normal_hbm, send_sem.at[5], recv_sem.at[5])
    for i, (buffer, count) in enumerate([(s1, LONS), (s3, LATS), (s4, LATS), (s6, LONS)]):
        drain(buffer, count, send_sem.at[(0, 2, 3, 5)[i]])
    second.wait_send()
    fifth.wait_send()
    for copy in halos:
        copy.wait_send()
    put_base.wait()
    keep.wait()
    drain(normal_hbm, LONS, recv_sem.at[5])


def finish(base_hbm, circles_hbm, jrad, out_hbm, normal, circles, base, sem):
    b = lax.axis_index("lat")
    get_circles = pltpu.make_async_copy(circles_hbm, circles, sem.at[0])
    get_circles.start()
    part = lambda v: pl.ds(v * INST, INST)
    gets = [
        pltpu.make_async_copy(base_hbm.at[part(v)], base.at[part(v)], sem.at[1 + v])
        for v in range(VARS)
    ]
    for copy in gets:
        copy.start()
    jr = [[jrad[v, w] for w in range(VARS)] for v in range(VARS)]
    row = lax.broadcasted_iota(jnp.int32, (8, 128), 0)
    get_circles.wait()
    for h in (0, 1):
        band = (16 * b + 8 * h + row).astype(f32)
        half_sine = 0.5 * jnp.sin((band + 0.5) * (math.pi / NLAT))
        rows = pl.ds(8 * h, 8)
        n = {}
        for v in range(VARS):
            value = {}
            for k in range(5):
                for kind in (0, 1) if k else (0,):
                    z, i = PLACE[v, k, kind]
                    value[k, kind] = circles[2 * z + h, pl.ds(8 * i, 8)]
            even = {k: value[k, 0] for k in range(1, 5)}
            odd = {k: value[k, 1] for k in range(1, 5)}
            c, s = fold_time(value[0, 0], even, odd)
            n[v, 0] = value[0, 0] + sum(even.values())
            for t in range(1, 5):
                n[v, t], n[v, 9 - t] = c[t] + s[t], c[t] - s[t]
        for v in range(VARS):
            for t in range(INST):
                normal[v * INST + t, rows] = n[v, t]
        for v in range(VARS):
            if h == 0:
                gets[v].wait()
            for t in range(INST):
                total = -n[v, t]
                for w in range(VARS):
                    total = total + jr[v][w] * n[w, t]
                at = v * INST + t
                base[at, 3, rows] = base[at, 3, rows] + half_sine * total
    puts = [
        pltpu.make_async_copy(base.at[part(v)], out_hbm.at[part(v)], sem.at[1 + v])
        for v in range(VARS)
    ]
    for copy in puts:
        copy.start()
    for copy in puts:
        copy.wait()


def shards(flow_state, jacobian_lat, jacobian_lon, jacobian_rad, ratio_real, ratio_imag, cut):
    x = flow_state.reshape(FIELDS, RAD, 16, 128)
    table = circle_table()
    small = np.zeros((56, 128), np.float32)
    small[0:16] = latitude_rows()
    small[16:32] = twiddle_table()
    small[48:50] = start_logs().reshape(2, 128)
    high, low = split_table(table)
    constants = [
        np.concatenate([np.ascontiguousarray(high.T), np.ascontiguousarray(low.T)], axis=1),
        np.concatenate([high, high, low]),
        small,
        ratio_rows().astype(np.float32),
    ]
    constants = [jnp.asarray(part) for part in constants]
    smem = pl.BlockSpec(memory_space=pltpu.SMEM)
    vmem = pl.BlockSpec(memory_space=pltpu.VMEM)
    hbm = pl.BlockSpec(memory_space=pl.ANY)
    v = lambda *shape: pltpu.VMEM(shape, f32)
    w = lambda *shape: pltpu.VMEM(shape, bf16)
    base, circles = pl.pallas_call(
        far_field,
        out_shape=[
            jax.ShapeDtypeStruct((FIELDS, RAD, 16, 128), f32),
            jax.ShapeDtypeStruct((16, ROWS, 128), f32),
        ],
        in_specs=[pl.BlockSpec(memory_space=pltpu.HBM)] * (7 + len(constants)),
        out_specs=[hbm, hbm],
        scratch_shapes=[
            v(FIELDS, 16, 128), v(FIELDS, RAD, 16, 128), v(FIELDS, RAD, 16, 128),
            v(16, ROWS, 128), v(16, ROWS, 128),
            v(2, 16, 8, 128), v(2, 16, 8, 128),
            v(32, 8, 128), v(32, 8, 128),
            v(32, 8, 128), v(32, 8, 128),
            v(2, 16, 8, 128), v(2, 16, 8, 128),
            v(16, ROWS, 128),
            v(2, 180, 128), v(2, 180, 128), v(2, 2, 16, 128), v(2, 2, 16, 128),
            v(256, 768), v(256, 768), v(4, MODES * 8, 128),
            w(8, 256, 256), w(8, 256, 256), w(8, 256, 256), w(8, 256, 256),
            v(4, MODES, 128), v(4, MODES, 128), v(4, MODES, 128), v(2, MODES, 128),
            w(768, 256), w(384, 768), v(56, 128), v(8, 16, 128),
            pltpu.SMEM((5, 5), f32), pltpu.SMEM((5, 5), f32), pltpu.SMEM((5, 5), f32),
            pltpu.SMEM((5,), jnp.int32), v(5, MODES), v(4, MODES),
            pltpu.SemaphoreType.DMA((6,)), pltpu.SemaphoreType.DMA((6,)),
            pltpu.SemaphoreType.DMA((4,)), pltpu.SemaphoreType.DMA((4,)),
            pltpu.SemaphoreType.DMA((12,)),
        ],
        compiler_params=pltpu.CompilerParams(
            collective_id=0, has_side_effects=True, vmem_limit_bytes=62 * 1024 * 1024
        ),
        name="far_field",
    )(x, jacobian_lat, jacobian_lon, jacobian_rad, cut, ratio_real.T, ratio_imag.T,
      *constants)
    residual, normal = pl.pallas_call(
        finish,
        out_shape=[
            jax.ShapeDtypeStruct((FIELDS, RAD, 16, 128), f32),
            jax.ShapeDtypeStruct((FIELDS, 16, 128), f32),
        ],
        in_specs=[hbm, hbm, smem],
        out_specs=[hbm, vmem],
        scratch_shapes=[
            v(16, ROWS, 128), v(FIELDS, RAD, 16, 128), pltpu.SemaphoreType.DMA((6,))
        ],
        compiler_params=pltpu.CompilerParams(vmem_limit_bytes=62 * 1024 * 1024),
        name="finish",
    )(base, circles, jacobian_rad)
    return (
        residual.reshape(VARS, INST, RAD, 16, 128),
        normal.reshape(VARS, INST, 16, 128),
    )


def solution(mesh):
    placed = (P(None, None, None, "lat", "lon"), P(), P(), P(), P(), P(), P())
    return jax.shard_map(
        shards,
        mesh=mesh,
        in_specs=placed,
        out_specs=(P(None, None, None, "lat", "lon"), P(None, None, "lat", "lon")),
        check_vma=False,
    )
```

```python
import functools
import math

import jax
import jax.numpy as jnp
import ml_dtypes
import numpy as np
from jax import lax
from jax.experimental import pallas as pl
from jax.experimental.pallas import tpu as pltpu
from jax.sharding import PartitionSpec as P

VARS, INST, RAD, NLAT, NLON, MODES = 5, 9, 4, 512, 2048, 256
FIELDS = VARS * INST
ROWS = 64
LATS, LONS = 32, 16
MESH = pl.DeviceIdType.MESH
f32, bf16 = jnp.float32, jnp.bfloat16
start_floor = -36.0


def split_table(table):
    high = table.astype(ml_dtypes.bfloat16)
    low = (table - high.astype(np.float64)).astype(ml_dtypes.bfloat16)
    return high, low


def circle_table():
    k = np.arange(128)
    table = np.zeros((LONS, 8, 3, 2, 128))
    for p in range(LONS):
        up = 2 * np.pi * p * k / 128
        down = -2 * np.pi * (p + 1) * k / 128
        rows = np.array(
            [
                [np.cos(up), np.sin(up)],
                [-np.sin(up), np.cos(up)],
                [np.cos(down), np.sin(down)],
                [np.sin(down), -np.cos(down)],
            ]
        )
        table[p, 0:4, 0] = rows
        table[p, 4:8, 1] = rows
        half = 2 * np.pi * (16 * p + 8) * k / 2048
        table[p, 4, 2, 0] = np.cos(up)
        table[p, 5, 2, 0] = -np.sin(up)
        table[p, 6, 2, 1] = np.cos(half)
        table[p, 7, 2, 1] = -np.sin(half)
    return table.reshape(LONS * 8, 768)


def twiddle_table():
    r = np.arange(8)[:, None]
    angle = 2 * np.pi * r * np.arange(128)[None] / 2048
    return np.concatenate([np.cos(angle), np.sin(angle)])


FOUR, THREE = (0, 5, 8, 13), (2, 3, 7, 10, 15)


def slot_table():
    pairs = [[(v, n, 0), (v, n, 1)] for v in range(VARS) for n in range(1, 5)]
    singles = [[(v, 0, 0)] for v in range(VARS)]
    slots = [pairs.pop() for _ in range(LONS)]
    for p in FOUR:
        slots[p] = slots[p] + pairs.pop()
    for p in THREE:
        slots[p] = slots[p] + singles.pop()
    return slots


SLOTS = slot_table()
PLACE = {item: (p, i) for p in range(LONS) for i, item in enumerate(SLOTS[p])}


def ratio_rows():
    rows = np.zeros((LONS, 16, 2, 4, 16))
    for p in range(LONS):
        for i, (_, n, part) in enumerate(SLOTS[p]):
            rows[p, n, :, i] = 2 / 9 if n else 1 / 9
            if n:
                rows[p, 7 + n, :, i] = -2 / 9 if part else 2 / 9
    return rows.reshape(LONS, 16, 128)


def fold_time(first, even, odd):
    c, s = {}, {}
    for n in range(1, 5):
        angles = {k: 2 * math.pi * n * k / 9 for k in range(1, 5)}
        c[n] = weigh([(1, first)] + [(math.cos(angles[k]), even[k]) for k in angles])
        s[n] = weigh([(math.sin(angles[k]), odd[k]) for k in angles])
    return c, s


def latitude_rows():
    column = np.arange(256)
    angle = (16 * (column // 8) + column % 8 + 0.5) * np.pi / NLAT
    angle = np.tile(angle.reshape(2, 128), (4, 1))
    return np.concatenate([np.cos(angle), np.sin(angle)])


def start_logs():
    return np.array(
        [
            0.5
            * (
                math.log((2 * m + 1) / (4 * math.pi))
                + math.lgamma(m + 0.5)
                - math.lgamma(m + 1.0)
                - 0.5 * math.log(math.pi)
            )
            for m in range(MODES)
        ]
    )


SPECTRAL = [0.5 * (-1) ** lag / math.sin(math.pi * lag / 9) for lag in range(1, 5)]


def split(value):
    high = value.astype(bf16)
    return high, (value - high.astype(f32)).astype(bf16)


def dot(a, b):
    return jnp.dot(a, b, preferred_element_type=f32)


def dot_wide(a, wide):
    total = dot(a[0], wide)
    return total[:, 0:128] + (total[:, 128:256] + dot(a[1], wide[:, 0:128]))


def weigh(terms):
    total = None
    for factor, value in terms:
        if abs(factor) < 1e-9:
            continue
        if abs(factor - 1) < 1e-9:
            total = value if total is None else total + value
        elif abs(factor + 1) < 1e-9:
            total = -value if total is None else total - value
        else:
            total = factor * value if total is None else total + factor * value
    return total


def sixteen(first, eighth, even, odd):
    cos = lambda n: math.cos(math.pi * n / 8)
    sin = lambda n: math.sin(math.pi * n / 8)
    plus, minus = first + eighth, first - eighth
    even_p = {d: even[d] + even[8 - d] for d in (1, 2, 3)}
    even_m = {d: even[d] - even[8 - d] for d in (1, 2, 3)}
    odd_p = {d: odd[d] + odd[8 - d] for d in (1, 2, 3)}
    odd_m = {d: odd[d] - odd[8 - d] for d in (1, 2, 3)}
    c, s = {}, {}
    for r in range(9):
        if r % 2 == 0:
            c[r] = weigh(
                [(1, plus), (cos(4 * r), even[4])] + [(cos(r * d), even_p[d]) for d in even_p]
            )
        else:
            c[r] = weigh([(1, minus)] + [(cos(r * d), even_m[d]) for d in even_m])
    for r in range(1, 8):
        if r % 2 == 0:
            s[r] = weigh([(sin(r * d), odd_m[d]) for d in odd_m])
        else:
            s[r] = weigh([(sin(4 * r), odd[4])] + [(sin(r * d), odd_p[d]) for d in odd_p])
    return c, s


def exchange(axis, me, count, send, recv, send_sem, recv_sem, rows=None):
    part = (lambda ref, i: ref.at[i]) if rows is None else (lambda ref, i: ref.at[i, rows])

    def one(step, carry):
        peer = lax.rem(me + step, count)
        pltpu.make_async_remote_copy(
            src_ref=part(send, peer),
            dst_ref=part(recv, me),
            send_sem=send_sem,
            recv_sem=recv_sem,
            device_id={axis: peer},
            device_id_type=MESH,
        ).start()
        return carry

    lax.fori_loop(1, count, one, 0)


def drain(buffer, count, sem, rows=None):
    part = buffer.at[pl.ds(0, count - 1)]
    if rows is not None:
        part = buffer.at[pl.ds(0, count - 1), pl.ds(0, rows)]
    pltpu.make_async_copy(part, part, sem).wait()


def mirrored(value):
    row = lax.broadcasted_iota(jnp.int32, (8, 128), 0)
    value = pltpu.roll(value, 4, 0)
    for bit in (2, 1):
        up, down = pltpu.roll(value, 8 - bit, 0), pltpu.roll(value, bit, 0)
        value = jnp.where((row & bit) == 0, up, down)
    return value


def far_field(
    x_hbm, jlat_hbm, jlon_hbm, jrad_hbm, cut_hbm, real_hbm, imag_hbm, fwd_hbm, inv_hbm, small_hbm,
    select_hbm, base_hbm, normal_hbm,
    shell, xv, base, s1, r1, s3, r3, s4, r4, s6,
    row_send, row_recv, col_send, col_recv,
    circles, lines, raw, t_h, t_l, tt_h, tt_l, grow, drop, seed, mult,
    fwd, inv, small, select, jlat, jlon, jrad, cut, real, imag,
    send_sem, recv_sem, halo_send, halo_recv, local,
):
    b = lax.axis_index("lat")
    p = lax.axis_index("lon")
    among = lambda group: functools.reduce(lambda a, c: a | c, [p == i for i in group])
    four, three = among(FOUR), among(THREE)
    two = jnp.logical_not(four | three)
    lower, upper, middle = pl.ds(0, 32), pl.ds(32, 32), pl.ds(32, 16)

    get_shell = pltpu.make_async_copy(x_hbm.at[:, 3], shell, local.at[0])
    get_shell.start()
    for d in range(LONS):
        r1[d, upper] = jnp.zeros((32, 128), f32)
    barrier = pltpu.get_barrier_semaphore()

    def greet(axis, me, count):
        def one(step, carry):
            pl.semaphore_signal(
                barrier, inc=1, device_id={axis: lax.rem(me + step, count)}, device_id_type=MESH
            )
            return carry

        lax.fori_loop(1, count, one, 0)

    greet("lon", p, LONS)
    greet("lat", b, LATS)

    get_all = pltpu.make_async_copy(x_hbm, xv, local.at[1])
    get_all.start()
    pairs = [
        (small_hbm, small), (real_hbm, real), (imag_hbm, imag), (cut_hbm, cut),
        (jlat_hbm, jlat), (jlon_hbm, jlon), (jrad_hbm, jrad),
        (select_hbm, select), (fwd_hbm, fwd), (inv_hbm, inv),
    ]
    tables = [
        pltpu.make_async_copy(src, dst, local.at[2 + i]) for i, (src, dst) in enumerate(pairs)
    ]
    for copy in tables:
        copy.start()

    get_shell.wait()
    for d in range(LONS):
        for i in range(len(SLOTS[d]), 4):
            s1[d, pl.ds(16 * i, 16)] = jnp.zeros((16, 128), f32)
    for v in range(VARS):
        q = [shell[v * INST + t] for t in range(INST)]
        even = {k: q[k] + q[9 - k] for k in range(1, 5)}
        odd = {k: q[k] - q[9 - k] for k in range(1, 5)}
        c, s = fold_time(q[0], even, odd)
        parts = {(v, 0, 0): q[0] + sum(even.values())}
        for n in range(1, 5):
            parts[v, n, 0], parts[v, n, 1] = c[n], s[n]
        for item, value in parts.items():
            d, i = PLACE[item]
            s1[d, pl.ds(16 * i, 16)] = value
    r1[p] = s1[p]
    pl.semaphore_wait(barrier, LONS + LATS - 2)
    for group, rows in ((FOUR, upper), (THREE, middle)):
        for peer in group:

            @pl.when(p != peer)
            def _():
                pltpu.make_async_remote_copy(
                    src_ref=s1.at[peer, rows],
                    dst_ref=r1.at[p, rows],
                    send_sem=send_sem.at[1],
                    recv_sem=recv_sem.at[1],
                    device_id={"lon": peer},
                    device_id_type=MESH,
                ).start()


    exchange("lon", p, LONS, s1, r1, send_sem.at[0], recv_sem.at[0], lower)

    get_all.wait()
    lane = lax.broadcasted_iota(jnp.int32, (16, 128), 1)
    row = lax.broadcasted_iota(jnp.int32, (16, 128), 0)
    x_rows = xv.reshape(FIELDS * RAD * 16, 128)
    row_send[0] = x_rows[pl.ds(0, 180, stride=16), :]
    row_send[1] = x_rows[pl.ds(15, 180, stride=16), :]

    def halo(axis, peer, index, send, recv):
        return pltpu.make_async_remote_copy(
            src_ref=send,
            dst_ref=recv,
            send_sem=halo_send.at[index],
            recv_sem=halo_recv.at[index],
            device_id={axis: peer},
            device_id_type=MESH,
        )

    halos = [
        halo("lat", lax.rem(b + LATS - 1, LATS), 0, row_send.at[0], row_recv.at[0]),
        halo("lat", lax.rem(b + 1, LATS), 1, row_send.at[1], row_recv.at[1]),
        halo("lon", lax.rem(p + LONS - 1, LONS), 2, col_send.at[0], col_recv.at[0]),
        halo("lon", lax.rem(p + 1, LONS), 3, col_send.at[1], col_recv.at[1]),
    ]
    halos[0].start()
    halos[1].start()

    q_own = b // 2
    orders = []
    for low in (0, 1):
        g = 2 * (b % 2) + low
        for s in (0, 1):
            r = 2 * g + 1 + s
            for t in (0, 1):
                m = 16 * q_own + r if t == 0 else 16 * q_own + 16 - r
                if s == 1:
                    m = jnp.where(g == 3, 16 * q_own + 8 * t, m)
                orders.append(m)
    for copy in tables:
        copy.wait()
    degree = lax.broadcasted_iota(jnp.int32, (MODES, 128), 0)
    deg = degree.astype(f32)
    cosine, sine_all = small[0:8], small[8:16]
    log_sine = jnp.log(sine_all)
    entry = lax.broadcasted_iota(jnp.int32, (2, 128), 0) * 128 + lax.broadcasted_iota(
        jnp.int32, (2, 128), 1
    )
    diagonals = []
    for mu, m in enumerate(orders):
        order = m.astype(f32)
        order2 = order * order

        def factor(d):
            return jnp.sqrt(
                jnp.maximum(4.0 * d * d - 1.0, 1.0) / jnp.maximum(d * d - order2, 1.0)
            )

        factor_now, factor_prev = factor(deg), factor(deg - 1.0)
        grow[mu] = jnp.where(degree > m, factor_now, 0.0)
        drop[mu] = jnp.where(degree > m + 1, factor_now / factor_prev, 0.0)
        seed[mu] = jnp.where(degree == m, 1.0, 0.0)
        log_start = jnp.where(entry == m, small[48:50], 0.0)
        log_start = jnp.sum(jnp.sum(log_start, axis=1, keepdims=True), axis=0, keepdims=True)
        log_diagonal = log_start + order * log_sine
        diagonals.append(
            jnp.where(
                log_diagonal >= start_floor, jnp.exp(jnp.maximum(log_diagonal, start_floor)), 0.0
            )
        )

    def advance(i, state):
        first = pl.multiple_of(i * 8, 8)
        at = pl.ds(first, 8)
        rows = [(grow[mu, at], drop[mu, at], seed[mu, at]) for mu in range(8)]
        state = list(state)
        for n in range(8):
            row_at = pl.ds(pl.multiple_of((first + n) * 8, 8), 8)
            for mu in range(8):
                a8, q8, d8 = rows[mu]
                latest, before = state[mu]
                step = a8[n : n + 1] * cosine
                rest = d8[n : n + 1] * diagonals[mu] - q8[n : n + 1] * before
                fresh = step * latest + rest
                raw[mu, row_at] = fresh
                state[mu] = (fresh, latest)
        return tuple(state)

    zero = jnp.zeros((8, 128), f32)
    lax.fori_loop(0, MODES // 8, advance, ((zero, zero),) * 8)
    for mu in range(8):
        for half in range(2):
            block = raw[mu, pl.ds(half, MODES, stride=8), :]
            high, low = split(block)
            t_h[mu, :, pl.ds(half * 128, 128)] = high
            t_l[mu, :, pl.ds(half * 128, 128)] = low
            high, low = split(block.T)
            tt_h[mu, pl.ds(half * 128, 128), :] = high
            tt_l[mu, pl.ds(half * 128, 128), :] = low

    lane_all = lax.broadcasted_iota(jnp.int32, (MODES, 128), 1)
    mu_lane = (lane_all // 2) % 8
    own = [mu_lane == mu for mu in range(8)]
    m_lane = jnp.zeros((MODES, 128), jnp.int32)
    for mu, m in enumerate(orders):
        m_lane = jnp.where(own[mu], m, m_lane)
    odd_lane = ((degree + m_lane) & 1 == 1) & (lane_all >= 64)
    mult[2] = jnp.where(odd_lane, -1.0, 1.0)
    w_lane = jnp.where(m_lane == 0, 1.0, 2.0) * mult[2]

    def by_degree(ratios, first, rows):
        count = ratios.shape[0]
        frequency = lax.broadcasted_iota(jnp.int32, (count, MODES), 0) + first
        last = jnp.zeros((count, MODES), jnp.int32)
        for n in range(first, 5):
            last = jnp.where(frequency == n, cut[n], last)
        kept = lax.broadcasted_iota(jnp.int32, (count, MODES), 1) <= last
        return lax.dot_general(
            jnp.where(kept, ratios[...], 0.0),
            rows,
            (((0,), (0,)), ((), ())),
            precision=lax.Precision.HIGHEST,
            preferred_element_type=f32,
        )

    mult[0] = by_degree(real, 0, select[p, 0:5]) * w_lane
    mult[1] = by_degree(imag, 1, select[p, 8:12]) * w_lane

    j_own = 16 * b + lax.broadcasted_iota(jnp.int32, (16, 256), 0)
    term = lax.broadcasted_iota(jnp.int32, (16, 256), 1) + 1
    angle = ((term * (2 * j_own + 1)) & (2 * NLAT - 1)).astype(f32) * (math.pi / NLAT)
    termf = term.astype(f32)
    series = jnp.sum(jnp.cos(angle) / (4.0 * termf * termf - 1.0), axis=1, keepdims=True)
    weight = (2.0 / NLAT) * (1.0 - 2.0 * series) * (2.0 * math.pi / NLON)
    weight = jnp.broadcast_to(weight, (16, 128))

    circles[pl.ds(0, 192), pl.ds(512, 256)] = jnp.zeros((192, 256), f32)
    circles[pl.ds(192, 64), pl.ds(256, 256)] = jnp.zeros((64, 256), f32)
    tw = lambda r: (small[16 + r : 17 + r], small[24 + r : 25 + r])
    drain(r1, LONS, recv_sem.at[0], 32)

    @pl.when(four)
    def _():
        drain(r1, LONS, recv_sem.at[1], 32)

    @pl.when(three)
    def _():
        drain(r1, LONS, recv_sem.at[1], 16)


    def analyse(i, carry):
        first = pl.multiple_of(i * 8, 8)
        x = [r1[d, pl.ds(first, 8)] for d in range(16)]
        even = {d: x[d] + x[16 - d] for d in range(1, 8)}
        odd = {d: x[d] - x[16 - d] for d in range(1, 8)}
        c, s = sixteen(x[0], x[8], even, odd)
        for r in range(1, 8):
            co, si = tw(r)
            at = pl.ds(64 * ((r - 1) // 2) + first, 8)
            column = 256 * ((r - 1) % 2)
            circles[at, pl.ds(column, 128)] = c[r] * co - s[r] * si
            circles[at, pl.ds(column + 128, 128)] = -s[r] * co - c[r] * si
        at = pl.ds(192 + first, 8)
        circles[at, pl.ds(512, 128)] = c[0]
        circles[at, pl.ds(640, 128)] = c[8]
        return carry

    lax.fori_loop(0, ROWS // 8, analyse, 0)
    found = dot_wide(split(circles[...]), fwd[...])
    lane8 = lax.broadcasted_iota(jnp.int32, (8, 128), 1)
    low_half = lane8 < 64
    granule = [lane8 // 8 == i for i in range(16)]

    def turn(value, granules):
        return pltpu.roll(value, (8 * granules) % 128, 1) if granules % 16 else value

    for side in (0, 1):
        tiles = []
        for h in (0, 1):
            for i in range(4):
                for low in (0, 1):
                    first = 64 * (2 * side + low) + 16 * i + 8 * h
                    tiles.append(found[first : first + 8] * weight[8 * h : 8 * h + 8])
        for q in range(16):
            message = turn(tiles[0], -q)
            for i in range(1, 16):
                message = jnp.where(granule[i], turn(tiles[i], i - q), message)
            s3[2 * q + side] = message
    r3[b] = s3[b]
    exchange("lat", b, LATS, s3, r3, send_sem.at[2], recv_sem.at[2])
    def pack(f, packed):
        packed = list(packed)
        for r in range(RAD):
            x = xv[f, r]
            at = f + 64 * (r % 2)
            here = lane == at
            for side in (0, 1):
                i = 2 * side + r // 2
                packed[i] = jnp.where(here, pltpu.roll(x, lax.rem(at + side, 128), 1), packed[i])
        return tuple(packed)

    packed = lax.fori_loop(0, FIELDS, pack, (jnp.zeros((16, 128), f32),) * 4)
    for i in range(4):
        col_send[i // 2, i % 2] = packed[i]
    halos[2].start()
    halos[3].start()

    drain(r3, LATS, recv_sem.at[2])

    folded = [jnp.where(low_half, r3[i], mirrored(r3[LATS - 1 - i])) for i in range(LATS)]
    wide = jnp.concatenate(split(jnp.concatenate(folded, axis=0)), axis=1)
    degrees = jnp.zeros((MODES, 128), f32)
    for i in range(8):
        degrees = jnp.where(own[i], dot_wide((t_h[i], t_l[i]), wide), degrees)
    degrees = degrees * mult[2]
    degrees = degrees + pltpu.roll(degrees, 64, 1)
    swapped = jnp.where(
        (lane_all // 16) % 2 == 0, pltpu.roll(degrees, 112, 1), pltpu.roll(degrees, 16, 1)
    )
    bent = mult[0] * degrees + mult[1] * swapped
    wide = jnp.concatenate(split(bent), axis=1)
    rows_out = jnp.zeros((256, 128), f32)
    for i in range(8):
        rows_out = jnp.where(own[i], dot_wide((tt_h[i], tt_l[i]), wide), rows_out)
    for i in range(LATS):
        here, there = rows_out[8 * i : 8 * i + 8], rows_out[248 - 8 * i : 256 - 8 * i]
        s4[i] = jnp.where(low_half, here, mirrored(there))
    r4[b] = s4[b]
    exchange("lat", b, LATS, s4, r4, send_sem.at[3], recv_sem.at[3])
    drain(r4, LATS, recv_sem.at[3])

    blocks = []
    for g in range(4):
        messages = [r4[2 * q + g // 2] for q in range(16)]
        for i in range(4):
            for h in (0, 1):
                at = 8 * h + 2 * i + g % 2
                tile = turn(messages[0], -at)
                for q in range(1, 16):
                    tile = jnp.where(granule[q], turn(messages[q], q - at), tile)
                blocks.append(tile)
    found = split(jnp.concatenate(blocks, axis=0))
    lines[...] = dot(jnp.concatenate(found, axis=1), inv[0:256]) + dot(found[0], inv[256:384])

    def synthesise(i, carry):
        first = pl.multiple_of(i * 8, 8)
        even, odd = {}, {}
        for r in range(1, 8):
            co, si = tw(r)
            at = pl.ds(64 * ((r - 1) // 2) + first, 8)
            column = 256 * ((r - 1) % 2)
            re, im = lines[at, pl.ds(column, 128)], lines[at, pl.ds(column + 128, 128)]
            even[r] = re * co - im * si
            odd[r] = re * si + im * co
        at = pl.ds(192 + first, 8)
        c, s = sixteen(lines[at, pl.ds(512, 128)], lines[at, pl.ds(640, 128)], even, odd)
        s6[0, pl.ds(first, 8)] = c[0]
        s6[8, pl.ds(first, 8)] = c[8]
        for d in range(1, 8):
            s6[d, pl.ds(first, 8)] = c[d] - s[d]
            s6[16 - d, pl.ds(first, 8)] = c[d] + s[d]
        return carry

    lax.fori_loop(0, ROWS // 8, synthesise, 0)
    keep = pltpu.make_async_copy(s6.at[p], normal_hbm.at[p], local.at[1])
    keep.start()
    parts = ((four, upper), (three, middle), (None, lower))
    for kind, rows in parts:
        send = lambda: exchange(
            "lon", p, LONS, s6, normal_hbm,
            send_sem.at[4 if kind is None else 5], recv_sem.at[4 if kind is None else 5], rows,
        )
        if kind is None:
            send()
        else:
            pl.when(kind)(send)
    for i in (2, 3, 0, 1):
        halos[i].wait_recv()
    band = (16 * b + row).astype(f32)
    sine = jnp.sin((band + 0.5) * (math.pi / NLAT))
    half_sine = 0.5 * sine
    south_keep = jnp.where(b == LATS - 1, 0.0, 1.0)
    north_keep = jnp.where(b == 0, 0.0, 1.0)
    jl = [[jlat[v, w] for w in range(VARS)] for v in range(VARS)]
    jo = [[jlon[v, w] for w in range(VARS)] for v in range(VARS)]
    jr = [[jrad[v, w] for w in range(VARS)] for v in range(VARS)]

    def one_instance(t, carry):
        for r in range(RAD):
            lat_d, rad_d, lon_d, rest = [], [], [], []
            for w in range(VARS):
                f = w * INST + t
                x = xv[f, r]
                index = f * RAD + r
                at = f + 64 * (r % 2)
                south_row = row_recv[0, pl.ds(index, 1)] * south_keep
                north_row = row_recv[1, pl.ds(index, 1)] * north_keep
                south = jnp.where(row == 15, south_row, pltpu.roll(x, 15, 0))
                north = jnp.where(row == 0, north_row, pltpu.roll(x, 1, 0))
                east_col = pltpu.roll(col_recv[0, r // 2], 127 - at, 1)
                west_col = pltpu.roll(col_recv[1, r // 2], lax.rem(128 - at, 128), 1)
                east = jnp.where(lane == 127, east_col, pltpu.roll(x, 127, 1))
                west = jnp.where(lane == 0, west_col, pltpu.roll(x, 1, 1))
                above = xv[f, r + 1] if r < RAD - 1 else x
                below = xv[f, r - 1] if r > 0 else jnp.zeros_like(x)
                lat_d.append(half_sine * (south - north))
                rad_d.append(half_sine * (above - below))
                lon_d.append(0.5 * (east - west))
                spread = half_sine * (south + north + above + below - 4.0 * x)
                timing = -spread - 0.5 * (east + west - 2.0 * x)
                for lag in range(1, 5):
                    back = xv[w * INST + lax.rem(t + 9 - lag, 9), r]
                    ahead = xv[w * INST + lax.rem(t + lag, 9), r]
                    timing = timing + SPECTRAL[lag - 1] * (back - ahead)
                rest.append(timing)
            for v in range(VARS):
                total = rest[v]
                for w in range(VARS):
                    total = total + (
                        jl[v][w] * lat_d[w] + jr[v][w] * rad_d[w] + jo[v][w] * lon_d[w]
                    )
                base[v * INST + t, r] = total
        return carry

    lax.fori_loop(0, INST, one_instance, 0)
    put_base = pltpu.make_async_copy(base, base_hbm, local.at[0])
    put_base.start()

    drain(s1, LONS, send_sem.at[0], 32)
    drain(s3, LATS, send_sem.at[2])
    drain(s4, LATS, send_sem.at[3])
    drain(s6, LONS, send_sem.at[4], 32)
    for kind, rows, blocks16 in ((four, 32, 11), (three, 16, 12), (two, 0, 13)):

        @pl.when(kind)
        def _():
            drain(s1, blocks16 + 1, send_sem.at[1], 16)
            if rows:
                drain(s6, LONS, send_sem.at[5], rows)
            drain(normal_hbm, blocks16 + 1, recv_sem.at[5], 16)

    for copy in halos:
        copy.wait_send()
    put_base.wait()
    keep.wait()
    drain(normal_hbm, LONS, recv_sem.at[4], 32)


def finish(base_hbm, circles_hbm, jrad, out_hbm, normal_hbm, circles, base, normal, change, sem):
    b = lax.axis_index("lat")
    get_circles = pltpu.make_async_copy(circles_hbm, circles, sem.at[0])
    get_circles.start()
    part = lambda v: pl.ds(v * INST, INST)
    gets = [
        pltpu.make_async_copy(base_hbm.at[part(v)], base.at[part(v)], sem.at[1 + v])
        for v in range(VARS)
    ]
    for copy in gets:
        copy.start()
    jr = [[jrad[v, w] for w in range(VARS)] for v in range(VARS)]
    row = lax.broadcasted_iota(jnp.int32, (8, 128), 0)
    puts = [
        pltpu.make_async_copy(base.at[part(v)], out_hbm.at[part(v)], sem.at[1 + v])
        for v in range(VARS)
    ]
    get_circles.wait()
    for h in (0, 1):
        band = (16 * b + 8 * h + row).astype(f32)
        half_sine = 0.5 * jnp.sin((band + 0.5) * (math.pi / NLAT))
        rows = pl.ds(8 * h, 8)
        n = {}
        for v in range(VARS):
            value = {}
            for k in range(5):
                for kind in (0, 1) if k else (0,):
                    p, i = PLACE[v, k, kind]
                    value[k, kind] = circles[p, pl.ds(16 * i + 8 * h, 8)]
            even = {k: value[k, 0] for k in range(1, 5)}
            odd = {k: value[k, 1] for k in range(1, 5)}
            c, s = fold_time(value[0, 0], even, odd)
            n[v, 0] = value[0, 0] + sum(even.values())
            for t in range(1, 5):
                n[v, t], n[v, 9 - t] = c[t] + s[t], c[t] - s[t]
        for v in range(VARS):
            for t in range(INST):
                normal[v * INST + t, rows] = n[v, t]
        if h == 1:
            put_normal = pltpu.make_async_copy(normal, normal_hbm, sem.at[6])
            put_normal.start()
        for v in range(VARS):
            for t in range(INST):
                total = -n[v, t]
                for w in range(VARS):
                    total = total + jr[v][w] * n[w, t]
                change[v * INST + t, rows] = half_sine * total
    for v in range(VARS):
        gets[v].wait()
        base[part(v), 3] = base[part(v), 3] + change[part(v)]
        puts[v].start()
    for copy in puts:
        copy.wait()
    put_normal.wait()


def shards(flow_state, jacobian_lat, jacobian_lon, jacobian_rad, ratio_real, ratio_imag, cut):
    x = flow_state.reshape(FIELDS, RAD, 16, 128)
    table = circle_table()
    small = np.zeros((56, 128), np.float32)
    small[0:16] = latitude_rows()
    small[16:32] = twiddle_table()
    small[48:50] = start_logs().reshape(2, 128)
    high, low = split_table(table)
    constants = [
        np.concatenate([np.ascontiguousarray(high.T), np.ascontiguousarray(low.T)], axis=1),
        np.concatenate([high, high, low]),
        small,
        ratio_rows().astype(np.float32),
    ]
    constants = [jnp.asarray(part) for part in constants]
    smem = pl.BlockSpec(memory_space=pltpu.SMEM)
    hbm = pl.BlockSpec(memory_space=pl.ANY)
    v = lambda *shape: pltpu.VMEM(shape, f32)
    w = lambda *shape: pltpu.VMEM(shape, bf16)
    base, circles = pl.pallas_call(
        far_field,
        out_shape=[
            jax.ShapeDtypeStruct((FIELDS, RAD, 16, 128), f32),
            jax.ShapeDtypeStruct((16, ROWS, 128), f32),
        ],
        in_specs=[pl.BlockSpec(memory_space=pltpu.HBM)] * (7 + len(constants)),
        out_specs=[hbm, hbm],
        scratch_shapes=[
            v(FIELDS, 16, 128), v(FIELDS, RAD, 16, 128), v(FIELDS, RAD, 16, 128),
            v(16, ROWS, 128), v(16, ROWS, 128),
            v(32, 8, 128), v(32, 8, 128),
            v(32, 8, 128), v(32, 8, 128),
            v(16, ROWS, 128),
            v(2, 180, 128), v(2, 180, 128), v(2, 2, 16, 128), v(2, 2, 16, 128),
            v(256, 768), v(256, 768), v(8, MODES * 8, 128),
            w(8, 256, 256), w(8, 256, 256), w(8, 256, 256), w(8, 256, 256),
            v(8, MODES, 128), v(8, MODES, 128), v(8, MODES, 128), v(3, MODES, 128),
            w(768, 256), w(384, 768), v(56, 128), v(16, 16, 128),
            pltpu.SMEM((5, 5), f32), pltpu.SMEM((5, 5), f32), pltpu.SMEM((5, 5), f32),
            pltpu.SMEM((5,), jnp.int32), v(5, MODES), v(4, MODES),
            pltpu.SemaphoreType.DMA((6,)), pltpu.SemaphoreType.DMA((6,)),
            pltpu.SemaphoreType.DMA((4,)), pltpu.SemaphoreType.DMA((4,)),
            pltpu.SemaphoreType.DMA((12,)),
        ],
        compiler_params=pltpu.CompilerParams(
            collective_id=0, has_side_effects=True, vmem_limit_bytes=62 * 1024 * 1024
        ),
        name="far_field",
    )(x, jacobian_lat, jacobian_lon, jacobian_rad, cut, ratio_real.T, ratio_imag.T,
      *constants)
    residual, normal = pl.pallas_call(
        finish,
        out_shape=[
            jax.ShapeDtypeStruct((FIELDS, RAD, 16, 128), f32),
            jax.ShapeDtypeStruct((FIELDS, 16, 128), f32),
        ],
        in_specs=[hbm, hbm, smem],
        out_specs=[hbm, hbm],
        scratch_shapes=[
            v(16, ROWS, 128), v(FIELDS, RAD, 16, 128), v(FIELDS, 16, 128),
            v(FIELDS, 16, 128), pltpu.SemaphoreType.DMA((7,)),
        ],
        compiler_params=pltpu.CompilerParams(vmem_limit_bytes=62 * 1024 * 1024),
        name="finish",
    )(base, circles, jacobian_rad)
    return (
        residual.reshape(VARS, INST, RAD, 16, 128),
        normal.reshape(VARS, INST, 16, 128),
    )


def solution(mesh):
    placed = (P(None, None, None, "lat", "lon"), P(), P(), P(), P(), P(), P())
    return jax.shard_map(
        shards,
        mesh=mesh,
        in_specs=placed,
        out_specs=(P(None, None, None, "lat", "lon"), P(None, None, "lat", "lon")),
        check_vma=False,
    )
```

```python
import functools
import math

import jax
import jax.numpy as jnp
import ml_dtypes
import numpy as np
from jax import lax
from jax.experimental import pallas as pl
from jax.experimental.pallas import tpu as pltpu
from jax.sharding import PartitionSpec as P

VARS, INST, RAD, NLAT, NLON, MODES = 5, 9, 4, 512, 2048, 256
FIELDS = VARS * INST
ROWS = 64
LATS, LONS = 32, 16
MESH = pl.DeviceIdType.MESH
f32, bf16 = jnp.float32, jnp.bfloat16
start_floor = -36.0


def split_table(table):
    high = table.astype(ml_dtypes.bfloat16)
    low = (table - high.astype(np.float64)).astype(ml_dtypes.bfloat16)
    return high, low


def circle_table():
    k = np.arange(128)
    table = np.zeros((LONS, 8, 3, 2, 128))
    for p in range(LONS):
        up = 2 * np.pi * p * k / 128
        down = -2 * np.pi * (p + 1) * k / 128
        rows = np.array(
            [
                [np.cos(up), np.sin(up)],
                [-np.sin(up), np.cos(up)],
                [np.cos(down), np.sin(down)],
                [np.sin(down), -np.cos(down)],
            ]
        )
        table[p, 0:4, 0] = rows
        table[p, 4:8, 1] = rows
        half = 2 * np.pi * (16 * p + 8) * k / 2048
        table[p, 4, 2, 0] = np.cos(up)
        table[p, 5, 2, 0] = -np.sin(up)
        table[p, 6, 2, 1] = np.cos(half)
        table[p, 7, 2, 1] = -np.sin(half)
    return table.reshape(LONS * 8, 768)


def twiddle_table():
    r = np.arange(8)[:, None]
    angle = 2 * np.pi * r * np.arange(128)[None] / 2048
    return np.concatenate([np.cos(angle), np.sin(angle)])


FOUR, THREE = (0, 9, 10, 15), (1, 8, 11, 13, 14)


def slot_table():
    pairs = [[(v, n, 0), (v, n, 1)] for v in range(VARS) for n in range(1, 5)]
    singles = [[(v, 0, 0)] for v in range(VARS)]
    slots = [pairs.pop() for _ in range(LONS)]
    for p in FOUR:
        slots[p] = slots[p] + pairs.pop()
    for p in THREE:
        slots[p] = slots[p] + singles.pop()
    return slots


SLOTS = slot_table()
PLACE = {item: (p, i) for p in range(LONS) for i, item in enumerate(SLOTS[p])}


def ratio_rows():
    rows = np.zeros((LONS, 16, 2, 4, 16))
    for p in range(LONS):
        for i, (_, n, part) in enumerate(SLOTS[p]):
            rows[p, n, :, i] = 2 / 9 if n else 1 / 9
            if n:
                rows[p, 7 + n, :, i] = -2 / 9 if part else 2 / 9
    return rows.reshape(LONS, 16, 128)


def fold_time(first, even, odd):
    c, s = {}, {}
    for n in range(1, 5):
        angles = {k: 2 * math.pi * n * k / 9 for k in range(1, 5)}
        c[n] = weigh([(1, first)] + [(math.cos(angles[k]), even[k]) for k in angles])
        s[n] = weigh([(math.sin(angles[k]), odd[k]) for k in angles])
    return c, s


def latitude_rows():
    column = np.arange(256)
    angle = (16 * (column // 8) + column % 8 + 0.5) * np.pi / NLAT
    angle = np.tile(angle.reshape(2, 128), (4, 1))
    return np.concatenate([np.cos(angle), np.sin(angle)])


def start_logs():
    return np.array(
        [
            0.5
            * (
                math.log((2 * m + 1) / (4 * math.pi))
                + math.lgamma(m + 0.5)
                - math.lgamma(m + 1.0)
                - 0.5 * math.log(math.pi)
            )
            for m in range(MODES)
        ]
    )


SPECTRAL = [0.5 * (-1) ** lag / math.sin(math.pi * lag / 9) for lag in range(1, 5)]


def split(value):
    high = value.astype(bf16)
    return high, (value - high.astype(f32)).astype(bf16)


def dot(a, b):
    return jnp.dot(a, b, preferred_element_type=f32)


def dot_wide(a, wide):
    total = dot(a[0], wide)
    return total[:, 0:128] + (total[:, 128:256] + dot(a[1], wide[:, 0:128]))


def weigh(terms):
    total = None
    for factor, value in terms:
        if abs(factor) < 1e-9:
            continue
        if abs(factor - 1) < 1e-9:
            total = value if total is None else total + value
        elif abs(factor + 1) < 1e-9:
            total = -value if total is None else total - value
        else:
            total = factor * value if total is None else total + factor * value
    return total


def sixteen(first, eighth, even, odd):
    cos = lambda n: math.cos(math.pi * n / 8)
    sin = lambda n: math.sin(math.pi * n / 8)
    plus, minus = first + eighth, first - eighth
    even_p = {d: even[d] + even[8 - d] for d in (1, 2, 3)}
    even_m = {d: even[d] - even[8 - d] for d in (1, 2, 3)}
    odd_p = {d: odd[d] + odd[8 - d] for d in (1, 2, 3)}
    odd_m = {d: odd[d] - odd[8 - d] for d in (1, 2, 3)}
    c, s = {}, {}
    for r in range(9):
        if r % 2 == 0:
            c[r] = weigh(
                [(1, plus), (cos(4 * r), even[4])] + [(cos(r * d), even_p[d]) for d in even_p]
            )
        else:
            c[r] = weigh([(1, minus)] + [(cos(r * d), even_m[d]) for d in even_m])
    for r in range(1, 8):
        if r % 2 == 0:
            s[r] = weigh([(sin(r * d), odd_m[d]) for d in odd_m])
        else:
            s[r] = weigh([(sin(4 * r), odd[4])] + [(sin(r * d), odd_p[d]) for d in odd_p])
    return c, s


def exchange(axis, me, count, send, recv, send_sem, recv_sem, rows=None):
    part = (lambda ref, i: ref.at[i]) if rows is None else (lambda ref, i: ref.at[i, rows])

    def one(step, carry):
        peer = lax.rem(me + step, count)
        pltpu.make_async_remote_copy(
            src_ref=part(send, peer),
            dst_ref=part(recv, me),
            send_sem=send_sem,
            recv_sem=recv_sem,
            device_id={axis: peer},
            device_id_type=MESH,
        ).start()
        return carry

    lax.fori_loop(1, count, one, 0)


def drain(buffer, count, sem, rows=None):
    part = buffer.at[pl.ds(0, count - 1)]
    if rows is not None:
        part = buffer.at[pl.ds(0, count - 1), pl.ds(0, rows)]
    pltpu.make_async_copy(part, part, sem).wait()


def mirrored(value):
    row = lax.broadcasted_iota(jnp.int32, (8, 128), 0)
    value = pltpu.roll(value, 4, 0)
    for bit in (2, 1):
        up, down = pltpu.roll(value, 8 - bit, 0), pltpu.roll(value, bit, 0)
        value = jnp.where((row & bit) == 0, up, down)
    return value


def far_field(
    x_hbm, jlat_hbm, jlon_hbm, jrad_hbm, cut_hbm, real_hbm, imag_hbm, fwd_hbm, inv_hbm, small_hbm,
    select_hbm, base_hbm, normal_hbm,
    shell, xv, base, s1, r1, s3, r3, s4, r4, s6,
    row_send, row_recv, col_send, col_recv,
    circles, lines, raw, t_h, t_l, tt_h, tt_l, grow, drop, seed, mult,
    fwd, inv, small, select, jlat, jlon, jrad, cut, real, imag,
    send_sem, recv_sem, halo_send, halo_recv, local,
):
    b = lax.axis_index("lat")
    p = lax.axis_index("lon")
    among = lambda group: functools.reduce(lambda a, c: a | c, [p == i for i in group])
    four, three = among(FOUR), among(THREE)
    two = jnp.logical_not(four | three)
    lower, upper, middle = pl.ds(0, 32), pl.ds(32, 32), pl.ds(32, 16)

    get_shell = pltpu.make_async_copy(x_hbm.at[:, 3], shell, local.at[0])
    get_shell.start()
    for d in range(LONS):
        r1[d, upper] = jnp.zeros((32, 128), f32)
    barrier = pltpu.get_barrier_semaphore()

    def greet(axis, me, count):
        def one(step, carry):
            pl.semaphore_signal(
                barrier, inc=1, device_id={axis: lax.rem(me + step, count)}, device_id_type=MESH
            )
            return carry

        lax.fori_loop(1, count, one, 0)

    greet("lon", p, LONS)
    greet("lat", b, LATS)

    get_all = pltpu.make_async_copy(x_hbm, xv, local.at[1])
    get_all.start()
    pairs = [
        (small_hbm, small), (real_hbm, real), (imag_hbm, imag), (cut_hbm, cut),
        (jlat_hbm, jlat), (jlon_hbm, jlon), (jrad_hbm, jrad),
        (select_hbm, select), (fwd_hbm, fwd), (inv_hbm, inv),
    ]
    tables = [
        pltpu.make_async_copy(src, dst, local.at[2 + i]) for i, (src, dst) in enumerate(pairs)
    ]
    for copy in tables:
        copy.start()

    get_shell.wait()
    for d in range(LONS):
        for i in range(len(SLOTS[d]), 4):
            s1[d, pl.ds(16 * i, 16)] = jnp.zeros((16, 128), f32)
    for v in range(VARS):
        q = [shell[v * INST + t] for t in range(INST)]
        even = {k: q[k] + q[9 - k] for k in range(1, 5)}
        odd = {k: q[k] - q[9 - k] for k in range(1, 5)}
        c, s = fold_time(q[0], even, odd)
        parts = {(v, 0, 0): q[0] + sum(even.values())}
        for n in range(1, 5):
            parts[v, n, 0], parts[v, n, 1] = c[n], s[n]
        for item, value in parts.items():
            d, i = PLACE[item]
            s1[d, pl.ds(16 * i, 16)] = value
    r1[p] = s1[p]
    pl.semaphore_wait(barrier, LONS + LATS - 2)
    exchange("lon", p, LONS, s1, r1, send_sem.at[0], recv_sem.at[0], lower)
    for group, rows in ((FOUR, upper), (THREE, middle)):
        for peer in group:

            @pl.when(p != peer)
            def _():
                pltpu.make_async_remote_copy(
                    src_ref=s1.at[peer, rows],
                    dst_ref=r1.at[p, rows],
                    send_sem=send_sem.at[1],
                    recv_sem=recv_sem.at[1],
                    device_id={"lon": peer},
                    device_id_type=MESH,
                ).start()


    get_all.wait()
    lane = lax.broadcasted_iota(jnp.int32, (16, 128), 1)
    row = lax.broadcasted_iota(jnp.int32, (16, 128), 0)
    x_rows = xv.reshape(FIELDS * RAD * 16, 128)
    row_send[0] = x_rows[pl.ds(0, 180, stride=16), :]
    row_send[1] = x_rows[pl.ds(15, 180, stride=16), :]

    def halo(axis, peer, index, send, recv):
        return pltpu.make_async_remote_copy(
            src_ref=send,
            dst_ref=recv,
            send_sem=halo_send.at[index],
            recv_sem=halo_recv.at[index],
            device_id={axis: peer},
            device_id_type=MESH,
        )

    halos = [
        halo("lat", lax.rem(b + LATS - 1, LATS), 0, row_send.at[0], row_recv.at[0]),
        halo("lat", lax.rem(b + 1, LATS), 1, row_send.at[1], row_recv.at[1]),
        halo("lon", lax.rem(p + LONS - 1, LONS), 2, col_send.at[0], col_recv.at[0]),
        halo("lon", lax.rem(p + 1, LONS), 3, col_send.at[1], col_recv.at[1]),
    ]
    halos[0].start()
    halos[1].start()

    q_own = b // 2
    orders = []
    for low in (0, 1):
        g = 2 * (b % 2) + low
        for s in (0, 1):
            r = 2 * g + 1 + s
            for t in (0, 1):
                m = 16 * q_own + r if t == 0 else 16 * q_own + 16 - r
                if s == 1:
                    m = jnp.where(g == 3, 16 * q_own + 8 * t, m)
                orders.append(m)
    for copy in tables:
        copy.wait()
    degree = lax.broadcasted_iota(jnp.int32, (MODES, 128), 0)
    deg = degree.astype(f32)
    cosine, sine_all = small[0:8], small[8:16]
    log_sine = jnp.log(sine_all)
    entry = lax.broadcasted_iota(jnp.int32, (2, 128), 0) * 128 + lax.broadcasted_iota(
        jnp.int32, (2, 128), 1
    )
    diagonals = []
    for mu, m in enumerate(orders):
        order = m.astype(f32)
        order2 = order * order

        def factor(d):
            return jnp.sqrt(
                jnp.maximum(4.0 * d * d - 1.0, 1.0) / jnp.maximum(d * d - order2, 1.0)
            )

        factor_now, factor_prev = factor(deg), factor(deg - 1.0)
        grow[mu] = jnp.where(degree > m, factor_now, 0.0)
        drop[mu] = jnp.where(degree > m + 1, factor_now / factor_prev, 0.0)
        seed[mu] = jnp.where(degree == m, 1.0, 0.0)
        log_start = jnp.where(entry == m, small[48:50], 0.0)
        log_start = jnp.sum(jnp.sum(log_start, axis=1, keepdims=True), axis=0, keepdims=True)
        log_diagonal = log_start + order * log_sine
        diagonals.append(
            jnp.where(
                log_diagonal >= start_floor, jnp.exp(jnp.maximum(log_diagonal, start_floor)), 0.0
            )
        )

    def advance(i, state):
        first = pl.multiple_of(i * 8, 8)
        at = pl.ds(first, 8)
        rows = [(grow[mu, at], drop[mu, at], seed[mu, at]) for mu in range(8)]
        state = list(state)
        for n in range(8):
            row_at = pl.ds(pl.multiple_of((first + n) * 8, 8), 8)
            for mu in range(8):
                a8, q8, d8 = rows[mu]
                latest, before = state[mu]
                step = a8[n : n + 1] * cosine
                rest = d8[n : n + 1] * diagonals[mu] - q8[n : n + 1] * before
                fresh = step * latest + rest
                raw[mu, row_at] = fresh
                state[mu] = (fresh, latest)
        return tuple(state)

    zero = jnp.zeros((8, 128), f32)
    lax.fori_loop(0, MODES // 8, advance, ((zero, zero),) * 8)
    for mu in range(8):
        for half in range(2):
            block = raw[mu, pl.ds(half, MODES, stride=8), :]
            high, low = split(block)
            t_h[mu, :, pl.ds(half * 128, 128)] = high
            t_l[mu, :, pl.ds(half * 128, 128)] = low
            high, low = split(block.T)
            tt_h[mu, pl.ds(half * 128, 128), :] = high
            tt_l[mu, pl.ds(half * 128, 128), :] = low

    lane_all = lax.broadcasted_iota(jnp.int32, (MODES, 128), 1)
    mu_lane = (lane_all // 2) % 8
    own = [mu_lane == mu for mu in range(8)]
    m_lane = jnp.zeros((MODES, 128), jnp.int32)
    for mu, m in enumerate(orders):
        m_lane = jnp.where(own[mu], m, m_lane)
    odd_lane = ((degree + m_lane) & 1 == 1) & (lane_all >= 64)
    mult[2] = jnp.where(odd_lane, -1.0, 1.0)
    w_lane = jnp.where(m_lane == 0, 1.0, 2.0) * mult[2]

    def by_degree(ratios, first, rows):
        count = ratios.shape[0]
        frequency = lax.broadcasted_iota(jnp.int32, (count, MODES), 0) + first
        last = jnp.zeros((count, MODES), jnp.int32)
        for n in range(first, 5):
            last = jnp.where(frequency == n, cut[n], last)
        kept = lax.broadcasted_iota(jnp.int32, (count, MODES), 1) <= last
        return lax.dot_general(
            jnp.where(kept, ratios[...], 0.0),
            rows,
            (((0,), (0,)), ((), ())),
            precision=lax.Precision.HIGHEST,
            preferred_element_type=f32,
        )

    mult[0] = by_degree(real, 0, select[p, 0:5]) * w_lane
    mult[1] = by_degree(imag, 1, select[p, 8:12]) * w_lane

    j_own = 16 * b + lax.broadcasted_iota(jnp.int32, (16, 256), 0)
    term = lax.broadcasted_iota(jnp.int32, (16, 256), 1) + 1
    angle = ((term * (2 * j_own + 1)) & (2 * NLAT - 1)).astype(f32) * (math.pi / NLAT)
    termf = term.astype(f32)
    series = jnp.sum(jnp.cos(angle) / (4.0 * termf * termf - 1.0), axis=1, keepdims=True)
    weight = (2.0 / NLAT) * (1.0 - 2.0 * series) * (2.0 * math.pi / NLON)
    weight = jnp.broadcast_to(weight, (16, 128))

    for k in (0, 1):
        circles[k, pl.ds(0, 96), pl.ds(512, 256)] = jnp.zeros((96, 256), f32)
        circles[k, pl.ds(96, 32), pl.ds(256, 256)] = jnp.zeros((32, 256), f32)
    tw = lambda r: (small[16 + r : 17 + r], small[24 + r : 25 + r])
    several = jnp.logical_not(two)
    lane8 = lax.broadcasted_iota(jnp.int32, (8, 128), 1)
    granule = [lane8 // 8 == i for i in range(16)]

    def turn(value, granules):
        return pltpu.roll(value, (8 * granules) % 128, 1) if granules % 16 else value

    def forward(k):
        def analyse(i, carry):
            first = pl.multiple_of(i * 8, 8)
            x = [r1[d, pl.ds(32 * k + first, 8)] for d in range(16)]
            even = {d: x[d] + x[16 - d] for d in range(1, 8)}
            odd = {d: x[d] - x[16 - d] for d in range(1, 8)}
            c, s = sixteen(x[0], x[8], even, odd)
            for r in range(1, 8):
                co, si = tw(r)
                at = pl.ds(32 * ((r - 1) // 2) + first, 8)
                column = 256 * ((r - 1) % 2)
                circles[k, at, pl.ds(column, 128)] = c[r] * co - s[r] * si
                circles[k, at, pl.ds(column + 128, 128)] = -s[r] * co - c[r] * si
            at = pl.ds(96 + first, 8)
            circles[k, at, pl.ds(512, 128)] = c[0]
            circles[k, at, pl.ds(640, 128)] = c[8]
            return carry

        lax.fori_loop(0, 4, analyse, 0)
        found = dot_wide(split(circles[k]), fwd[...])
        for side in (0, 1):
            tiles = {}
            for h in (0, 1):
                for i in (0, 1):
                    for low in (0, 1):
                        first = 32 * (2 * side + low) + 16 * i + 8 * h
                        tile = found[first : first + 8] * weight[8 * h : 8 * h + 8]
                        tiles[8 * h + 2 * (2 * k + i) + low] = tile
            for q in range(16):
                to = 2 * q + side
                message = s3[to] if k else jnp.zeros((8, 128), f32)
                for i, tile in tiles.items():
                    message = jnp.where(granule[i], turn(tile, i - q), message)
                s3[to] = message

    def keep(k):
        rows = pl.ds(32 * k, 32)
        return pltpu.make_async_copy(s6.at[p, rows], normal_hbm.at[p, rows], local.at[2 + k])

    def backward(k):
        blocks = []
        for g in range(4):
            messages = [r4[2 * q + g // 2] for q in range(16)]
            for i in (0, 1):
                for h in (0, 1):
                    at = 8 * h + 2 * (2 * k + i) + g % 2
                    tile = turn(messages[0], -at)
                    for q in range(1, 16):
                        tile = jnp.where(granule[q], turn(messages[q], q - at), tile)
                    blocks.append(tile)
        found = split(jnp.concatenate(blocks, axis=0))
        lines[k] = dot(jnp.concatenate(found, axis=1), inv[0:256]) + dot(found[0], inv[256:384])

        def synthesise(i, carry):
            first = pl.multiple_of(i * 8, 8)
            even, odd = {}, {}
            for r in range(1, 8):
                co, si = tw(r)
                at = pl.ds(32 * ((r - 1) // 2) + first, 8)
                column = 256 * ((r - 1) % 2)
                re, im = lines[k, at, pl.ds(column, 128)], lines[k, at, pl.ds(column + 128, 128)]
                even[r] = re * co - im * si
                odd[r] = re * si + im * co
            at = pl.ds(96 + first, 8)
            c, s = sixteen(lines[k, at, pl.ds(512, 128)], lines[k, at, pl.ds(640, 128)], even, odd)
            to = pl.ds(32 * k + first, 8)
            s6[0, to] = c[0]
            s6[8, to] = c[8]
            for d in range(1, 8):
                s6[d, to] = c[d] - s[d]
                s6[16 - d, to] = c[d] + s[d]
            return carry

        lax.fori_loop(0, 4, synthesise, 0)
        keep(k).start()

    def send_circles(k, rows):
        exchange(
            "lon", p, LONS, s6, normal_hbm, send_sem.at[6 + k], recv_sem.at[6 + k], rows
        )

    drain(r1, LONS, recv_sem.at[0], 32)
    forward(0)

    @pl.when(four)
    def _():
        drain(r1, LONS, recv_sem.at[1], 32)

    @pl.when(three)
    def _():
        drain(r1, LONS, recv_sem.at[1], 16)

    @pl.when(several)
    def _():
        forward(1)

    r3[b] = s3[b]
    exchange("lat", b, LATS, s3, r3, send_sem.at[2], recv_sem.at[2])
    def pack(f, packed):
        packed = list(packed)
        for r in range(RAD):
            x = xv[f, r]
            at = f + 64 * (r % 2)
            here = lane == at
            for side in (0, 1):
                i = 2 * side + r // 2
                packed[i] = jnp.where(here, pltpu.roll(x, lax.rem(at + side, 128), 1), packed[i])
        return tuple(packed)

    packed = lax.fori_loop(0, FIELDS, pack, (jnp.zeros((16, 128), f32),) * 4)
    for i in range(4):
        col_send[i // 2, i % 2] = packed[i]
    halos[2].start()
    halos[3].start()

    drain(r3, LATS, recv_sem.at[2])

    low_half = lane8 < 64
    folded = [jnp.where(low_half, r3[i], mirrored(r3[LATS - 1 - i])) for i in range(LATS)]
    wide = jnp.concatenate(split(jnp.concatenate(folded, axis=0)), axis=1)
    degrees = jnp.zeros((MODES, 128), f32)
    for i in range(8):
        degrees = jnp.where(own[i], dot_wide((t_h[i], t_l[i]), wide), degrees)
    degrees = degrees * mult[2]
    degrees = degrees + pltpu.roll(degrees, 64, 1)
    swapped = jnp.where(
        (lane_all // 16) % 2 == 0, pltpu.roll(degrees, 112, 1), pltpu.roll(degrees, 16, 1)
    )
    bent = mult[0] * degrees + mult[1] * swapped
    wide = jnp.concatenate(split(bent), axis=1)
    rows_out = jnp.zeros((256, 128), f32)
    for i in range(8):
        rows_out = jnp.where(own[i], dot_wide((tt_h[i], tt_l[i]), wide), rows_out)
    for i in range(LATS):
        here, there = rows_out[8 * i : 8 * i + 8], rows_out[248 - 8 * i : 256 - 8 * i]
        s4[i] = jnp.where(low_half, here, mirrored(there))
    r4[b] = s4[b]
    exchange("lat", b, LATS, s4, r4, send_sem.at[3], recv_sem.at[3])
    drain(r4, LATS, recv_sem.at[3])

    backward(0)
    send_circles(0, lower)

    @pl.when(several)
    def _():
        backward(1)

    @pl.when(four)
    def _():
        send_circles(1, upper)

    @pl.when(three)
    def _():
        send_circles(1, middle)

    for i in (2, 3, 0, 1):
        halos[i].wait_recv()
    band = (16 * b + row).astype(f32)
    sine = jnp.sin((band + 0.5) * (math.pi / NLAT))
    half_sine = 0.5 * sine
    south_keep = jnp.where(b == LATS - 1, 0.0, 1.0)
    north_keep = jnp.where(b == 0, 0.0, 1.0)
    jl = [[jlat[v, w] for w in range(VARS)] for v in range(VARS)]
    jo = [[jlon[v, w] for w in range(VARS)] for v in range(VARS)]
    jr = [[jrad[v, w] for w in range(VARS)] for v in range(VARS)]

    def one_instance(t, carry):
        for r in range(RAD):
            lat_d, rad_d, lon_d, rest = [], [], [], []
            for w in range(VARS):
                f = w * INST + t
                x = xv[f, r]
                index = f * RAD + r
                at = f + 64 * (r % 2)
                south_row = row_recv[0, pl.ds(index, 1)] * south_keep
                north_row = row_recv[1, pl.ds(index, 1)] * north_keep
                south = jnp.where(row == 15, south_row, pltpu.roll(x, 15, 0))
                north = jnp.where(row == 0, north_row, pltpu.roll(x, 1, 0))
                east_col = pltpu.roll(col_recv[0, r // 2], 127 - at, 1)
                west_col = pltpu.roll(col_recv[1, r // 2], lax.rem(128 - at, 128), 1)
                east = jnp.where(lane == 127, east_col, pltpu.roll(x, 127, 1))
                west = jnp.where(lane == 0, west_col, pltpu.roll(x, 1, 1))
                above = xv[f, r + 1] if r < RAD - 1 else x
                below = xv[f, r - 1] if r > 0 else jnp.zeros_like(x)
                lat_d.append(half_sine * (south - north))
                rad_d.append(half_sine * (above - below))
                lon_d.append(0.5 * (east - west))
                spread = half_sine * (south + north + above + below - 4.0 * x)
                timing = -spread - 0.5 * (east + west - 2.0 * x)
                for lag in range(1, 5):
                    back = xv[w * INST + lax.rem(t + 9 - lag, 9), r]
                    ahead = xv[w * INST + lax.rem(t + lag, 9), r]
                    timing = timing + SPECTRAL[lag - 1] * (back - ahead)
                rest.append(timing)
            for v in range(VARS):
                total = rest[v]
                for w in range(VARS):
                    total = total + (
                        jl[v][w] * lat_d[w] + jr[v][w] * rad_d[w] + jo[v][w] * lon_d[w]
                    )
                base[v * INST + t, r] = total
        return carry

    lax.fori_loop(0, INST, one_instance, 0)
    put_base = pltpu.make_async_copy(base, base_hbm, local.at[0])
    put_base.start()

    drain(s1, LONS, send_sem.at[0], 32)
    drain(s3, LATS, send_sem.at[2])
    drain(s4, LATS, send_sem.at[3])
    drain(s6, LONS, send_sem.at[6], 32)
    keep(0).wait()
    for kind, rows, blocks16 in ((four, 32, 11), (three, 16, 12), (two, 0, 13)):

        @pl.when(kind)
        def _():
            drain(s1, blocks16 + 1, send_sem.at[1], 16)
            if rows:
                drain(s6, LONS, send_sem.at[7], rows)
                keep(1).wait()
            drain(normal_hbm, blocks16 + 1, recv_sem.at[7], 16)

    for copy in halos:
        copy.wait_send()
    put_base.wait()
    drain(normal_hbm, LONS, recv_sem.at[6], 32)


def finish(base_hbm, circles_hbm, jrad, out_hbm, normal_hbm, circles, base, normal, change, sem):
    b = lax.axis_index("lat")
    get_circles = pltpu.make_async_copy(circles_hbm, circles, sem.at[0])
    get_circles.start()
    part = lambda v: pl.ds(v * INST, INST)
    gets = [
        pltpu.make_async_copy(base_hbm.at[part(v)], base.at[part(v)], sem.at[1 + v])
        for v in range(VARS)
    ]
    for copy in gets:
        copy.start()
    jr = [[jrad[v, w] for w in range(VARS)] for v in range(VARS)]
    row = lax.broadcasted_iota(jnp.int32, (8, 128), 0)
    puts = [
        pltpu.make_async_copy(base.at[part(v)], out_hbm.at[part(v)], sem.at[1 + v])
        for v in range(VARS)
    ]
    get_circles.wait()
    for h in (0, 1):
        band = (16 * b + 8 * h + row).astype(f32)
        half_sine = 0.5 * jnp.sin((band + 0.5) * (math.pi / NLAT))
        rows = pl.ds(8 * h, 8)
        n = {}
        for v in range(VARS):
            value = {}
            for k in range(5):
                for kind in (0, 1) if k else (0,):
                    p, i = PLACE[v, k, kind]
                    value[k, kind] = circles[p, pl.ds(16 * i + 8 * h, 8)]
            even = {k: value[k, 0] for k in range(1, 5)}
            odd = {k: value[k, 1] for k in range(1, 5)}
            c, s = fold_time(value[0, 0], even, odd)
            n[v, 0] = value[0, 0] + sum(even.values())
            for t in range(1, 5):
                n[v, t], n[v, 9 - t] = c[t] + s[t], c[t] - s[t]
        for v in range(VARS):
            for t in range(INST):
                normal[v * INST + t, rows] = n[v, t]
        if h == 1:
            put_normal = pltpu.make_async_copy(normal, normal_hbm, sem.at[6])
            put_normal.start()
        for v in range(VARS):
            for t in range(INST):
                total = -n[v, t]
                for w in range(VARS):
                    total = total + jr[v][w] * n[w, t]
                change[v * INST + t, rows] = half_sine * total
    for v in range(VARS):
        gets[v].wait()
        base[part(v), 3] = base[part(v), 3] + change[part(v)]
        puts[v].start()
    for copy in puts:
        copy.wait()
    put_normal.wait()


def shards(flow_state, jacobian_lat, jacobian_lon, jacobian_rad, ratio_real, ratio_imag, cut):
    x = flow_state.reshape(FIELDS, RAD, 16, 128)
    table = circle_table()
    small = np.zeros((56, 128), np.float32)
    small[0:16] = latitude_rows()
    small[16:32] = twiddle_table()
    small[48:50] = start_logs().reshape(2, 128)
    high, low = split_table(table)
    constants = [
        np.concatenate([np.ascontiguousarray(high.T), np.ascontiguousarray(low.T)], axis=1),
        np.concatenate([high, high, low]),
        small,
        ratio_rows().astype(np.float32),
    ]
    constants = [jnp.asarray(part) for part in constants]
    smem = pl.BlockSpec(memory_space=pltpu.SMEM)
    hbm = pl.BlockSpec(memory_space=pl.ANY)
    v = lambda *shape: pltpu.VMEM(shape, f32)
    w = lambda *shape: pltpu.VMEM(shape, bf16)
    base, circles = pl.pallas_call(
        far_field,
        out_shape=[
            jax.ShapeDtypeStruct((FIELDS, RAD, 16, 128), f32),
            jax.ShapeDtypeStruct((16, ROWS, 128), f32),
        ],
        in_specs=[pl.BlockSpec(memory_space=pltpu.HBM)] * (7 + len(constants)),
        out_specs=[hbm, hbm],
        scratch_shapes=[
            v(FIELDS, 16, 128), v(FIELDS, RAD, 16, 128), v(FIELDS, RAD, 16, 128),
            v(16, ROWS, 128), v(16, ROWS, 128),
            v(32, 8, 128), v(32, 8, 128),
            v(32, 8, 128), v(32, 8, 128),
            v(16, ROWS, 128),
            v(2, 180, 128), v(2, 180, 128), v(2, 2, 16, 128), v(2, 2, 16, 128),
            v(2, 128, 768), v(2, 128, 768), v(8, MODES * 8, 128),
            w(8, 256, 256), w(8, 256, 256), w(8, 256, 256), w(8, 256, 256),
            v(8, MODES, 128), v(8, MODES, 128), v(8, MODES, 128), v(3, MODES, 128),
            w(768, 256), w(384, 768), v(56, 128), v(16, 16, 128),
            pltpu.SMEM((5, 5), f32), pltpu.SMEM((5, 5), f32), pltpu.SMEM((5, 5), f32),
            pltpu.SMEM((5,), jnp.int32), v(5, MODES), v(4, MODES),
            pltpu.SemaphoreType.DMA((8,)), pltpu.SemaphoreType.DMA((8,)),
            pltpu.SemaphoreType.DMA((4,)), pltpu.SemaphoreType.DMA((4,)),
            pltpu.SemaphoreType.DMA((12,)),
        ],
        compiler_params=pltpu.CompilerParams(
            collective_id=0, has_side_effects=True, vmem_limit_bytes=62 * 1024 * 1024
        ),
        name="far_field",
    )(x, jacobian_lat, jacobian_lon, jacobian_rad, cut, ratio_real.T, ratio_imag.T,
      *constants)
    residual, normal = pl.pallas_call(
        finish,
        out_shape=[
            jax.ShapeDtypeStruct((FIELDS, RAD, 16, 128), f32),
            jax.ShapeDtypeStruct((FIELDS, 16, 128), f32),
        ],
        in_specs=[hbm, hbm, smem],
        out_specs=[hbm, hbm],
        scratch_shapes=[
            v(16, ROWS, 128), v(FIELDS, RAD, 16, 128), v(FIELDS, 16, 128),
            v(FIELDS, 16, 128), pltpu.SemaphoreType.DMA((7,)),
        ],
        compiler_params=pltpu.CompilerParams(vmem_limit_bytes=62 * 1024 * 1024),
        name="finish",
    )(base, circles, jacobian_rad)
    return (
        residual.reshape(VARS, INST, RAD, 16, 128),
        normal.reshape(VARS, INST, 16, 128),
    )


def solution(mesh):
    placed = (P(None, None, None, "lat", "lon"), P(), P(), P(), P(), P(), P())
    return jax.shard_map(
        shards,
        mesh=mesh,
        in_specs=placed,
        out_specs=(P(None, None, None, "lat", "lon"), P(None, None, "lat", "lon")),
        check_vma=False,
    )
```
